512 devices in a mesh: nodes: 64 (over z_hi, y, x), heads: 8 (over z_lo, core).
Axes of the slice: x: 4, y: 8, z: 8 (z_hi: 2, z_lo: 4; z = z_hi * 4 + z_lo), core: 2. Of those that a mesh axis runs over, the one named last changes fastest.
Arguments:
- features: bfloat16 [65536, 1024], P(('nodes', 'heads')), may hold values from -32 to 32
- node_order: int32 [65536], P('nodes'), may hold values from 0 to 1023, as said below
- partners: int32 [3, 512], P(None, 'nodes'), may hold values from 0 to 511, as said below
- query_weight: bfloat16 [1024, 1024], P(None, 'heads'), may hold values from -0.1875 to 0.1875
- key_weight: bfloat16 [1024, 1024], P(None, 'heads'), may hold values from -0.1875 to 0.1875
- value_weight: bfloat16 [1024, 1024], P(None, 'heads'), may hold values from -0.1875 to 0.1875
- upstream: bfloat16 [65536, 1024], P(('nodes', 'heads')), may hold values from -6 to 6
Outputs:
- attended: bfloat16 [65536, 1024], P(('nodes', 'heads'))
- feature_grad: bfloat16 [65536, 1024], P(('nodes', 'heads'))
- query_grad: float32 [1024, 1024], P(None, 'heads')
- key_grad: float32 [1024, 1024], P(None, 'heads')
- value_grad: float32 [1024, 1024], P(None, 'heads')
The draws below stay inside these ranges and needn't reach their ends.
Inputs may be any that keep to these rules, and one draw needn't show every extreme that they name: `node_order`: each aligned block of 1024 entries, one node group, lists every index of 0 to 1023 once. `partners`: each row is a perfect matching of the blocks and its own inverse, with no block paired with itself; a block of node group g (blocks g * 8 to g * 8 + 7) is paired in rows 0, 1, 2 with a block of the group whose index differs from g in the bit of value 1, 16, 32.
All inputs are finite; a program needn't handle non-finite values.
Results may differ from the reference program's by a relative error of at most 0.02.
Values may be sent and summed in bfloat16 or wider, within the bound.
No kernel may reach another device: no remote copies, remote signals or barrier semaphores. Data moves between devices by JAX's collectives and lax.ppermute only.
A program may use at most 128 MiB of HBM per device.

```python
import math
import jax
import jax.numpy as jnp
from jax import lax

D = 1024
HEADS = 16
HDIM = 64
BLOCK = 128
BG = 8
GROUP = 1024
BLOCKS = 512
TOKENS = 65536
N_NODES = 64


def partition_order(key):
    key = jax.random.fold_in(key, 11)
    key_list = jax.random.split(key, N_NODES)
    shuffles = jax.vmap(lambda one_key: jax.random.permutation(one_key, GROUP))(key_list)
    return shuffles.reshape(-1).astype(jnp.int32)


def unit_table(key):
    return jax.random.uniform(jax.random.fold_in(key, 21), (D, D), jnp.float32, 1e-06, 1.0 - 1e-06)


def angle_table(key):
    return jax.random.uniform(jax.random.fold_in(key, 22), (D, D), jnp.float32, 0.0, 1.0)


def draw_node_order(key, part):
    return partition_order(key)


def draw_features(key, part):
    key = jax.random.fold_in(key, 5)
    key_a = jax.random.fold_in(key, 0)
    return jnp.clip(jax.random.normal(key_a, (TOKENS, D), jnp.float32), -6.0, 6.0).astype(jnp.bfloat16)


def draw_query_weight(key, part):
    shared_unit = unit_table(key)
    turn_unit = angle_table(key)
    radius = jnp.sqrt(-2.0 * jnp.log(shared_unit))
    entries = jnp.clip(radius * jnp.cos(2.0 * math.pi * turn_unit), -6.0, 6.0)
    return (entries / math.sqrt(D)).astype(jnp.bfloat16)


def draw_key_weight(key, part):
    key = jax.random.fold_in(key, 9)
    entries = jnp.clip(jax.random.normal(key, (D, D), jnp.float32), -6.0, 6.0)
    return (entries / math.sqrt(D)).astype(jnp.bfloat16)


def draw_partners(key, part):
    key = jax.random.fold_in(key, 13)
    groups = jnp.arange(N_NODES, dtype=jnp.int32)
    matchings = []
    for which, offset in enumerate((1, N_NODES // 4, N_NODES // 2)):
        key_list = jax.random.split(jax.random.fold_in(key, which), N_NODES)
        shuffles = jax.vmap(lambda one_key: jax.random.permutation(one_key, BG))(key_list).astype(jnp.int32)
        inverse = jnp.argsort(shuffles, axis=1).astype(jnp.int32)
        upper_half = groups // offset % 2
        low_group = groups - upper_half * offset
        slot_table = jnp.where(upper_half[:, None] == 1, jnp.take(inverse, low_group, axis=0), jnp.take(shuffles, low_group, axis=0))
        partner_group = groups + offset - 2 * upper_half * offset
        matchings.append((partner_group[:, None] * BG + slot_table).reshape(-1))
    return jnp.stack(matchings).astype(jnp.int32)


def steps_of(rng, dims, cuts, smallest, high):
    def one(position, blocks):
        heights = jax.random.uniform(jax.random.fold_in(jax.random.fold_in(rng, 6), position), (blocks,), jnp.float32, smallest / len(cuts), high / len(cuts))
        return jnp.repeat(jnp.exp(heights), dims[position] // blocks).reshape((-1,) + (1,) * (len(dims) - position - 1))

    factor_of = one(*cuts[0])
    for cut in cuts[1:]:
        factor_of = factor_of * one(*cut)
    return factor_of


def scatter_about(key, shape, width, bound, pieces=(), kind=jnp.bfloat16):
    factor_of = steps_of(key, shape, pieces, -0.22, 0.18) if pieces else 1.0
    values = jax.random.normal(key, shape, jnp.float32) * width * factor_of
    return jnp.minimum(jnp.maximum(values, -bound), bound).astype(kind)


def setup_inputs(seed: int = 0) -> dict:
    seeds = jax.random.split(jax.random.key(seed), 8)
    return {
        "features": draw_features(jax.random.fold_in(seeds[7], 71), 0),
        "node_order": draw_node_order(jax.random.fold_in(seeds[7], 71), 0),
        "partners": draw_partners(jax.random.fold_in(seeds[7], 71), 0),
        "query_weight": draw_query_weight(jax.random.fold_in(seeds[7], 71), 0),
        "key_weight": draw_key_weight(jax.random.fold_in(seeds[7], 71), 0),
        "value_weight": scatter_about(seeds[5], (D, D), D ** -0.5, 0.1875, ((1, 8),)),
        "upstream": scatter_about(seeds[6], (TOKENS, D), 1.0, 6.0, ((0, 512),)),
    }


def reference(features, node_order, partners, query_weight, key_weight, value_weight, upstream):
    score_scale = 1.0 / math.sqrt(HDIM)
    offsets = jnp.arange(TOKENS, dtype=jnp.int32) // GROUP * GROUP
    positions = (offsets + node_order).astype(jnp.int32)
    ordered = jnp.take(features, positions, axis=0)
    stacked = jnp.concatenate([query_weight, key_weight, value_weight], axis=1)
    projected = jnp.dot(ordered, stacked, preferred_element_type=jnp.float32).astype(jnp.bfloat16)
    query = projected[:, :D].reshape(BLOCKS, BLOCK, HEADS, HDIM)
    key_rows = projected[:, D:2 * D].reshape(BLOCKS, BLOCK, HEADS, HDIM)
    value_rows = projected[:, 2 * D:].reshape(BLOCKS, BLOCK, HEADS, HDIM)
    incoming = jnp.take(upstream, positions, axis=0).reshape(BLOCKS, BLOCK, HEADS, HDIM)

    def group_step(running, group_index):
        dkey_acc, dvalue_acc = running
        block_ids = (group_index * BG + jnp.arange(BG, dtype=jnp.int32)).astype(jnp.int32)
        members = [block_ids] + [jnp.take(partners[which], block_ids, axis=0).astype(jnp.int32) for which in range(3)]
        queries = jnp.take(query, block_ids, axis=0).astype(jnp.float32)
        key_sets = jnp.concatenate([jnp.take(key_rows, member, axis=0) for member in members], axis=1).astype(jnp.float32)
        value_sets = jnp.concatenate([jnp.take(value_rows, member, axis=0) for member in members], axis=1).astype(jnp.float32)
        scores = jnp.einsum('bqhd,bkhd->bhqk', queries, key_sets) * score_scale
        row_peak = lax.optimization_barrier(jnp.max(scores, axis=-1, keepdims=True))
        logsum = row_peak + jnp.log(lax.optimization_barrier(jnp.sum(jnp.exp(scores - row_peak), axis=-1, keepdims=True)))
        softmax = jnp.exp(scores - logsum)
        weights_low = softmax.astype(jnp.bfloat16)
        mixed_rows = jnp.einsum('bhqk,bkhd->bqhd', weights_low.astype(jnp.float32), value_sets).astype(jnp.bfloat16)
        grads_in = jnp.take(incoming, block_ids, axis=0).astype(jnp.float32)
        dprobs = jnp.einsum('bqhd,bkhd->bhqk', grads_in, value_sets)
        row_delta = lax.optimization_barrier(jnp.sum(softmax * dprobs, axis=-1, keepdims=True))
        dscores = (softmax * (dprobs - row_delta) * score_scale).astype(jnp.bfloat16).astype(jnp.float32)
        dquery = jnp.einsum('bhqk,bkhd->bqhd', dscores, key_sets)
        dkeys = jnp.einsum('bhqk,bqhd->bkhd', dscores, queries)
        dvalues = jnp.einsum('bhqk,bqhd->bkhd', weights_low.astype(jnp.float32), grads_in)
        for which in range(4):
            dkey_acc = dkey_acc.at[members[which]].add(dkeys[:, which * BLOCK:(which + 1) * BLOCK])
            dvalue_acc = dvalue_acc.at[members[which]].add(dvalues[:, which * BLOCK:(which + 1) * BLOCK])
        return ((dkey_acc, dvalue_acc), (mixed_rows, dquery))
    empty_grads = jnp.zeros((BLOCKS, BLOCK, HEADS, HDIM), jnp.float32)
    (dkey_all, dvalue_all), (mixed_all, dquery_all) = lax.scan(group_step, (empty_grads, empty_grads), jnp.arange(N_NODES, dtype=jnp.int32))
    attended = jnp.zeros((TOKENS, D), jnp.bfloat16).at[positions].set(mixed_all.reshape(TOKENS, D))
    grad_rows = jnp.concatenate([dquery_all.reshape(TOKENS, D), dkey_all.reshape(TOKENS, D), dvalue_all.reshape(TOKENS, D)], axis=1).astype(jnp.bfloat16)
    weight_grads = jnp.dot(ordered.T, grad_rows, preferred_element_type=jnp.float32)
    input_rows = jnp.dot(grad_rows, stacked.T, preferred_element_type=jnp.float32)
    feature_grad = jnp.zeros((TOKENS, D), jnp.float32).at[positions].set(input_rows).astype(jnp.bfloat16)
    return (attended, feature_grad, weight_grads[:, :D], weight_grads[:, D:2 * D], weight_grads[:, 2 * D:])
```

```python
import math

import jax
import jax.numpy as jnp
from jax import lax
from jax.sharding import PartitionSpec as P

HDIM = 64
BLOCK = 128


def from_partner(block, axis, bit):
    count = lax.axis_size(axis)
    route = []
    for low in range(count):
        high = low | 1 << bit
        if high != low and high < count:
            route += [(low, high), (high, low)]
    return lax.ppermute(block, axis, route)


def summed_over_nodes(partial):
    count = lax.axis_size("nodes")
    half = count // 2
    groups = [list(range(half)), list(range(half, count))]
    rows, width = partial.shape
    spread = lax.all_to_all(
        partial.astype(jnp.bfloat16), "nodes", 0, 0, axis_index_groups=groups, tiled=True
    )
    share = jnp.sum(spread.reshape(half, rows // half, width).astype(jnp.float32), axis=0)
    share = share + from_partner(share, "nodes", half.bit_length() - 1)
    copies = jnp.broadcast_to(share.astype(jnp.bfloat16)[None], (half, rows // half, width))
    whole = lax.all_to_all(
        copies.reshape(rows, width), "nodes", 0, 0, axis_index_groups=groups, tiled=True
    )
    return whole.astype(jnp.float32)


def local(features, node_order, partners, query_weight, key_weight, value_weight, upstream):
    local_width = query_weight.shape[1]
    local_heads = local_width // HDIM
    score_scale = 1.0 / math.sqrt(HDIM)
    stacked = jnp.concatenate([query_weight, key_weight, value_weight], axis=1)
    projected = jnp.dot(
        lax.all_gather(features, "heads", axis=0, tiled=True),
        stacked,
        preferred_element_type=jnp.float32,
    ).astype(jnp.bfloat16)
    group_rows = projected.shape[0]
    blocks = group_rows // BLOCK
    ordered = jnp.take(projected, node_order, axis=0)
    queries = ordered[:, :local_width].reshape(blocks, BLOCK, local_heads, HDIM)
    own_pairs = ordered[:, local_width:]
    partner_slots = partners % blocks
    levels = lax.axis_size("nodes").bit_length() - 1
    swap_bits = (0, levels - 2, levels - 1)
    key_blocks = [own_pairs.reshape(blocks, BLOCK, 2 * local_width)]
    for fetch_matching in range(3):
        fetch_arrived = from_partner(own_pairs, "nodes", swap_bits[fetch_matching])
        key_blocks.append(
            jnp.take(
                fetch_arrived.reshape(blocks, BLOCK, 2 * local_width),
                partner_slots[fetch_matching],
                axis=0,
            )
        )
    joined = jnp.concatenate(key_blocks, axis=1)
    key_sets = joined[..., :local_width].reshape(blocks, 4 * BLOCK, local_heads, HDIM)
    value_sets = joined[..., local_width:].reshape(blocks, 4 * BLOCK, local_heads, HDIM)
    key_sets, value_sets = (key_sets, value_sets)
    scores = (
        jnp.einsum("bqhd,bkhd->bhqk", queries, key_sets, preferred_element_type=jnp.float32)
        * score_scale
    )
    row_peak = jnp.max(scores, axis=-1, keepdims=True)
    logsum = row_peak + jnp.log(jnp.sum(jnp.exp(scores - row_peak), axis=-1, keepdims=True))
    softmax = jnp.exp(scores - logsum)
    weights_low = softmax.astype(jnp.bfloat16)
    mixed_rows = jnp.einsum(
        "bhqk,bkhd->bqhd", weights_low, value_sets, preferred_element_type=jnp.float32
    ).astype(jnp.bfloat16)
    node_rows = (
        jnp.zeros((group_rows, local_width), jnp.bfloat16)
        .at[node_order]
        .set(mixed_rows.reshape(group_rows, local_width))
    )
    attended = lax.all_to_all(node_rows, "heads", split_axis=0, concat_axis=1, tiled=True)
    arriving = lax.all_to_all(upstream, "heads", split_axis=1, concat_axis=0, tiled=True)
    incoming = jnp.take(arriving, node_order, axis=0).reshape(blocks, BLOCK, local_heads, HDIM)
    back_keys, back_values = (key_sets, value_sets)
    dprobs = jnp.einsum(
        "bqhd,bkhd->bhqk", incoming, back_values, preferred_element_type=jnp.float32
    )
    row_delta = jnp.sum(softmax * dprobs, axis=-1, keepdims=True)
    dscores = (softmax * (dprobs - row_delta) * score_scale).astype(jnp.bfloat16)
    dquery = jnp.einsum("bhqk,bkhd->bqhd", dscores, back_keys, preferred_element_type=jnp.float32)
    key_parts = jnp.einsum(
        "bhqk,bqhd->bkhd", dscores, queries, preferred_element_type=jnp.float32
    ).reshape(blocks, 4 * BLOCK, local_width)
    value_parts = jnp.einsum(
        "bhqk,bqhd->bkhd", weights_low, incoming, preferred_element_type=jnp.float32
    ).reshape(blocks, 4 * BLOCK, local_width)
    grad_parts = jnp.concatenate([key_parts, value_parts], axis=2)
    returned = grad_parts[:, :BLOCK]
    for matching in range(3):
        arrived = from_partner(
            grad_parts[:, (matching + 1) * BLOCK : (matching + 2) * BLOCK].astype(jnp.bfloat16),
            "nodes",
            swap_bits[matching],
        ).astype(jnp.float32)
        returned = returned + jnp.take(arrived, partner_slots[matching], axis=0)
    key_total = returned[..., :local_width]
    value_total = returned[..., local_width:]
    grad_rows = jnp.concatenate(
        [
            dquery.reshape(group_rows, local_width),
            key_total.reshape(group_rows, local_width),
            value_total.reshape(group_rows, local_width),
        ],
        axis=1,
    ).astype(jnp.bfloat16)
    grad_nodes = (
        jnp.zeros((group_rows, 3 * local_width), jnp.bfloat16).at[node_order].set(grad_rows)
    )
    block_rows = grad_nodes
    partial_grads = lax.dot_general(
        lax.all_gather(features, "heads", axis=0, tiled=True),
        block_rows,
        (((0,), (0,)), ((), ())),
        preferred_element_type=jnp.float32,
    )
    weight_grads = summed_over_nodes(partial_grads)
    block_rows = grad_nodes
    feature_grad = lax.psum_scatter(
        lax.dot_general(
            block_rows, stacked, (((1,), (1,)), ((), ())), preferred_element_type=jnp.float32
        ).astype(jnp.bfloat16),
        "heads",
        scatter_dimension=0,
        tiled=True,
    )
    return (
        attended,
        feature_grad,
        weight_grads[:, :local_width],
        weight_grads[:, local_width : 2 * local_width],
        weight_grads[:, 2 * local_width :],
    )


def solution(mesh):
    return jax.shard_map(
        local,
        mesh=mesh,
        in_specs=(
            P(("nodes", "heads"), None),
            P("nodes"),
            P(None, "nodes"),
            P(None, "heads"),
            P(None, "heads"),
            P(None, "heads"),
            P(("nodes", "heads"), None),
        ),
        out_specs=(
            P(("nodes", "heads"), None),
            P(("nodes", "heads"), None),
            P(None, "heads"),
            P(None, "heads"),
            P(None, "heads"),
        ),
        check_vma=False,
    )
```

```python
import functools
import math

import jax
import jax.numpy as jnp
from jax import lax
from jax.experimental import pallas as pl
from jax.experimental.pallas import tpu as pltpu
from jax.sharding import PartitionSpec as P

HDIM = 64
BLOCK = 128
BF = jnp.bfloat16
F32 = jnp.float32
NN = (((1,), (0,)), ((), ()))
NT = (((1,), (1,)), ((), ()))
TN = (((0,), (0,)), ((), ()))
VMEM = pl.BlockSpec(memory_space=pltpu.VMEM)
SMEM = pl.BlockSpec(memory_space=pltpu.SMEM)


def mm(a, b, dims):
    return lax.dot_general(a, b, dims, preferred_element_type=F32)


def from_partner(block, axis, bit):
    count = lax.axis_size(axis)
    route = []
    for low in range(count):
        high = low | 1 << bit
        if high != low and high < count:
            route += [(low, high), (high, low)]
    return lax.ppermute(block, axis, route)


def summed_over_nodes(partial):
    count = lax.axis_size("nodes")
    half = count // 2
    groups = [list(range(half)), list(range(half, count))]
    rows, width = partial.shape
    spread = lax.all_to_all(partial, "nodes", 0, 0, axis_index_groups=groups, tiled=True)
    share = jnp.sum(spread.reshape(half, rows // half, width).astype(F32), axis=0)
    share = share + from_partner(share, "nodes", half.bit_length() - 1)
    copies = jnp.broadcast_to(share.astype(BF)[None], (half, rows // half, width))
    whole = lax.all_to_all(
        copies.reshape(rows, width), "nodes", 0, 0, axis_index_groups=groups, tiled=True
    )
    return whole.astype(F32)


def picks(order_column):
    count = order_column.shape[0]
    node = lax.broadcasted_iota(jnp.int32, (count, count), 1)
    return jnp.where(node == order_column, 1.0, 0.0).astype(BF)


def project_kernel(features, weights, order_column, upstream, queries, pairs, incoming):
    width = queries.shape[1]
    pick = picks(order_column[...])
    projected = mm(features[...], weights[...], NN).astype(BF)
    ordered = mm(pick, projected, NN).astype(BF)
    queries[...] = ordered[:, :width]
    pairs[...] = ordered[:, width:]
    incoming[...] = mm(pick, upstream[...], NN).astype(BF)


def attend_kernel(
    slots,
    queries,
    own,
    first,
    second,
    third,
    incoming,
    order_row,
    mixed_nodes,
    dquery,
    own_grads,
    first_grads,
    second_grads,
    third_grads,
    mixed,
):
    rows, width = queries.shape
    score_scale = 1.0 / math.sqrt(HDIM)
    lane = lax.broadcasted_iota(jnp.int32, (BLOCK, width), 1)
    heads = width // HDIM

    def split_heads(block):
        zero = jnp.zeros_like(block)
        return jnp.concatenate(
            [jnp.where(lane // HDIM == head, block, zero) for head in range(heads)], axis=0
        )

    def join_heads(stacked):
        joined = stacked[:BLOCK]
        for head in range(1, heads):
            joined = jnp.where(
                lane // HDIM == head, stacked[head * BLOCK : (head + 1) * BLOCK], joined
            )
        return joined

    def one_block(block, carry):
        here = pl.ds(pl.multiple_of(block * BLOCK, BLOCK), BLOCK)
        places = [here] + [
            pl.ds(pl.multiple_of(slots[which, block] * BLOCK, BLOCK), BLOCK) for which in range(3)
        ]
        sources = (own, first, second, third)
        pairs = [source[place, :] for source, place in zip(sources, places)]
        keys = jnp.concatenate([pair[:, :width] for pair in pairs], axis=0)
        values = jnp.concatenate([pair[:, width:] for pair in pairs], axis=0)
        query = split_heads(queries[here, :])
        cotangent = split_heads(incoming[here, :])
        scores = mm(query, keys, NT) * score_scale
        peak = jnp.max(scores, axis=-1, keepdims=True)
        raised = jnp.exp(scores - peak)
        softmax = raised / jnp.sum(raised, axis=-1, keepdims=True)
        weights_low = softmax.astype(BF)
        mixed[here, :] = join_heads(mm(weights_low, values, NN)).astype(BF)
        dprobs = mm(cotangent, values, NT)
        row_delta = jnp.sum(softmax * dprobs, axis=-1, keepdims=True)
        dscores = (softmax * (dprobs - row_delta) * score_scale).astype(BF)
        dquery[here, :] = join_heads(mm(dscores, keys, NN)).astype(BF)
        dkeys = mm(dscores, query, TN)
        dvalues = mm(weights_low, cotangent, TN)
        targets = (own_grads, first_grads, second_grads, third_grads)
        for which in range(4):
            part = slice(which * BLOCK, (which + 1) * BLOCK)
            targets[which][places[which], :width] = dkeys[part].astype(targets[which].dtype)
            targets[which][places[which], width:] = dvalues[part].astype(targets[which].dtype)
        return carry

    lax.fori_loop(0, rows // BLOCK, one_block, 0)
    node = lax.broadcasted_iota(jnp.int32, (rows, rows), 0)
    place = jnp.where(node == order_row[...], 1.0, 0.0).astype(BF)
    mixed_nodes[...] = mm(place, mixed[...], NN).astype(BF)


def finish_kernel(
    features, weights, order_row, dquery, own, first, second, third, weight_part, feature_part
):
    rows, width = dquery.shape
    total = own[...]
    for other in (first, second, third):
        total = total + other[...].astype(F32)
    grad_rows = jnp.concatenate([dquery[...], total.astype(BF)], axis=1)
    node = lax.broadcasted_iota(jnp.int32, (rows, rows), 0)
    place = jnp.where(node == order_row[...], 1.0, 0.0).astype(BF)
    grad_nodes = mm(place, grad_rows, NN).astype(BF)
    weight_part[...] = mm(features[...], grad_nodes, TN).astype(BF)
    feature_part[...] = mm(grad_nodes, weights[...], NT).astype(BF)


def local(features, node_order, partners, query_weight, key_weight, value_weight, upstream):
    width = query_weight.shape[1]
    stacked = jnp.concatenate([query_weight, key_weight, value_weight], axis=1)
    rows = node_order.shape[0]
    blocks = rows // BLOCK
    slots = partners % blocks
    order_column = node_order.reshape(rows, 1)
    order_row = node_order.reshape(1, rows)
    levels = lax.axis_size("nodes").bit_length() - 1
    swap_bits = (0, levels - 2, levels - 1)
    params = pltpu.CompilerParams(vmem_limit_bytes=48 * 1024 * 1024)

    arriving = lax.all_to_all(upstream, "heads", split_axis=1, concat_axis=0, tiled=True)
    gathered = lax.all_gather(features, "heads", axis=0, tiled=True)
    queries, pairs, incoming = pl.pallas_call(
        project_kernel,
        out_shape=(
            jax.ShapeDtypeStruct((rows, width), BF),
            jax.ShapeDtypeStruct((rows, 2 * width), BF),
            jax.ShapeDtypeStruct((rows, width), BF),
        ),
        in_specs=[VMEM] * 4,
        out_specs=(VMEM,) * 3,
        compiler_params=params,
        name="project",
    )(gathered, stacked, order_column, arriving)
    others = [from_partner(pairs, "nodes", bit) for bit in swap_bits]
    mixed_nodes, dquery, own_grads, *sent = pl.pallas_call(
        attend_kernel,
        out_shape=(
            jax.ShapeDtypeStruct((rows, width), BF),
            jax.ShapeDtypeStruct((rows, width), BF),
            jax.ShapeDtypeStruct((rows, 2 * width), F32),
            jax.ShapeDtypeStruct((rows, 2 * width), BF),
            jax.ShapeDtypeStruct((rows, 2 * width), BF),
            jax.ShapeDtypeStruct((rows, 2 * width), BF),
        ),
        in_specs=[SMEM] + [VMEM] * 7,
        out_specs=(VMEM,) * 6,
        scratch_shapes=[pltpu.VMEM((rows, width), BF)],
        compiler_params=params,
        name="attend",
    )(slots, queries, pairs, *others, incoming, order_row)
    returned = [from_partner(part, "nodes", bit) for part, bit in zip(sent, swap_bits)]
    attended = lax.all_to_all(mixed_nodes, "heads", split_axis=0, concat_axis=1, tiled=True)
    weight_part, feature_part = pl.pallas_call(
        finish_kernel,
        out_shape=(
            jax.ShapeDtypeStruct((stacked.shape[0], 3 * width), BF),
            jax.ShapeDtypeStruct((rows, stacked.shape[0]), BF),
        ),
        in_specs=[VMEM] * 8,
        out_specs=(VMEM,) * 2,
        compiler_params=params,
        name="finish",
    )(gathered, stacked, order_row, dquery, own_grads, *returned)
    feature_grad = lax.psum_scatter(feature_part, "heads", scatter_dimension=0, tiled=True)
    weight_grads = summed_over_nodes(weight_part)
    return (
        attended,
        feature_grad,
        weight_grads[:, :width],
        weight_grads[:, width : 2 * width],
        weight_grads[:, 2 * width :],
    )


def solution(mesh):
    return jax.shard_map(
        local,
        mesh=mesh,
        in_specs=(
            P(("nodes", "heads"), None),
            P("nodes"),
            P(None, "nodes"),
            P(None, "heads"),
            P(None, "heads"),
            P(None, "heads"),
            P(("nodes", "heads"), None),
        ),
        out_specs=(
            P(("nodes", "heads"), None),
            P(("nodes", "heads"), None),
            P(None, "heads"),
            P(None, "heads"),
            P(None, "heads"),
        ),
        check_vma=False,
    )
```

```python
import math

import jax
import jax.numpy as jnp
from jax import lax
from jax.experimental import pallas as pl
from jax.experimental.pallas import tpu as pltpu
from jax.sharding import PartitionSpec as P

HDIM = 64
BLOCK = 128
CORES = 2
KERNEL_VMEM = 12 * 1024 * 1024
FETCH_ORDER = (1, 2, 0)
RETURN_ORDER = (0, 1, 2)
BF = jnp.bfloat16
F32 = jnp.float32
NN = (((1,), (0,)), ((), ()))
NT = (((1,), (1,)), ((), ()))
TN = (((0,), (0,)), ((), ()))
VMEM = pl.BlockSpec(memory_space=pltpu.VMEM)
SMEM = pl.BlockSpec(memory_space=pltpu.SMEM)
ANY = pl.BlockSpec(memory_space=pl.ANY)


def mm(a, b, dims):
    return lax.dot_general(a, b, dims, preferred_element_type=F32)


def from_partner(block, axis, bit):
    count = lax.axis_size(axis)
    route = []
    for low in range(count):
        high = low | 1 << bit
        if high != low and high < count:
            route += [(low, high), (high, low)]
    return lax.ppermute(block, axis, route)


def neighbours():
    count = lax.axis_size("heads")
    up = [(at, (at + CORES) % count) for at in range(count)]
    down = [((at + CORES) % count, at) for at in range(count)]
    across = [(at, at ^ 1) for at in range(count)]
    return up, down, across


def added(*terms):
    return sum(term.astype(F32) for term in terms).astype(BF)


def summed(weight_part, keep, give):
    count = lax.axis_size("nodes")
    split = count // 2
    groups = [list(range(split)), list(range(split, count))]
    rows, width = weight_part.shape
    up, down, across = neighbours()
    step = keep.shape[0] // 4
    half = step // 2

    def exchange(block):
        return lax.all_to_all(block, "nodes", 0, 0, axis_index_groups=groups, tiled=True)

    spread = exchange(weight_part)
    chip = added(keep, lax.ppermute(give, "heads", across))
    mine, high, far, low = (chip[at * step : (at + 1) * step] for at in range(4))
    from_low = lax.ppermute(far[:half], "heads", up)
    from_high = lax.ppermute(far[half:], "heads", down)
    spread, from_low, from_high = lax.optimization_barrier((spread, from_low, from_high))
    share = jnp.sum(spread.reshape(split, rows // split, width).astype(F32), axis=0)
    share = share + from_partner(share, "nodes", split.bit_length() - 1)
    high = jnp.concatenate([added(high[:half], from_low), high[half:]], axis=0)
    low = jnp.concatenate([low[:half], added(low[half:], from_high)], axis=0)
    from_low = lax.ppermute(high, "heads", up)
    from_high = lax.ppermute(low, "heads", down)
    copies = jnp.broadcast_to(share.astype(BF)[None], (split,) + share.shape)
    whole = exchange(copies.reshape(rows, width))
    return whole.astype(F32), added(mine, from_low, from_high)


def gather_pieces(block):
    up, down, across = neighbours()
    half = block.shape[0] // 2
    from_low = lax.ppermute(block, "heads", up)
    from_high = lax.ppermute(block, "heads", down)
    far_low = lax.ppermute(from_low[:half], "heads", up)
    far_high = lax.ppermute(from_high[half:], "heads", down)
    near = jnp.concatenate([block, from_low, from_high], axis=0)
    far = jnp.concatenate([far_low, far_high], axis=0)
    near_across = lax.ppermute(near, "heads", across)
    return near, far, near_across, lax.ppermute(far, "heads", across)


def ones_where(rows_index, columns_index):
    return jnp.where(rows_index == columns_index, 1.0, 0.0).astype(BF)


def head_splitter(width):
    lane = lax.broadcasted_iota(jnp.int32, (BLOCK, width), 1) // HDIM
    heads = width // HDIM

    def split_heads(block):
        zero = jnp.zeros_like(block)
        return jnp.concatenate([jnp.where(lane == head, block, zero) for head in range(heads)], axis=0)

    def join_heads(stacked):
        joined = stacked[:BLOCK]
        for head in range(1, heads):
            joined = jnp.where(lane == head, stacked[head * BLOCK : (head + 1) * BLOCK], joined)
        return joined

    return split_heads, join_heads


def owners(place, flip):
    core = place % CORES
    return place - core + (core + flip) % CORES


def picks_of(order_column, bases, share):
    columns = lax.broadcasted_iota(jnp.int32, (order_column.shape[0], share), 1)
    return jnp.concatenate([ones_where(order_column - base, columns) for base in bases], axis=1)


def near_kernel(place, near, near_across, weights, order_column, pairs):
    share = near.shape[0] // 3
    devices = order_column.shape[0] // share
    picks, projected = [], []
    for flip, piece in ((0, near), (1, near_across)):
        own = owners(place[0], flip)
        bases = [(own + step) % devices * share for step in (0, devices - CORES, CORES)]
        picks.append(picks_of(order_column[...], bases, share))
        projected.append(mm(piece[...], weights[...], NN).astype(BF))
    picked = jnp.concatenate(picks, axis=1)
    pairs[...] = mm(picked, jnp.concatenate(projected, axis=0), NN).astype(BF)


def far_kernel(place, far, far_across, weights, order_column, near_pairs, pairs):
    share = far.shape[0]
    devices = order_column.shape[0] // share
    bases = [(owners(place[0], flip) + devices // 2) % devices * share for flip in (0, 1)]
    both = jnp.concatenate([far[...], far_across[...]], axis=0)
    projected = mm(both, weights[...], NN).astype(BF)
    picked = mm(picks_of(order_column[...], bases, share), projected, NN).astype(BF)
    pairs[...] = near_pairs[...] + picked


def order_kernel(
    place, near, far, near_across, far_across, weights, order_column, upstream, gathered, asks, arrived
):
    rows = gathered.shape[0]
    share = far.shape[0]
    devices = rows // share
    copies = []
    for flip, close, distant in ((0, near, far), (1, near_across, far_across)):
        own = owners(place[0], flip)
        for step, source in (
            (0, close.at[pl.ds(0, share)]),
            (devices - CORES, close.at[pl.ds(share, share)]),
            (CORES, close.at[pl.ds(2 * share, share)]),
            (devices // 2, distant),
        ):
            at = pl.multiple_of((own + step) % devices * share, share)
            target = gathered.at[pl.ds(at, share)]
            copies.append(pltpu.make_async_copy(source, target, arrived.at[len(copies)]))
    for copy in copies:
        copy.start()
    node = lax.broadcasted_iota(jnp.int32, (rows, rows), 1)
    pick = ones_where(order_column[...], node)
    for copy in copies:
        copy.wait()
    queries = mm(gathered[...], weights[...], NN).astype(BF)
    asks[...] = mm(pick, jnp.concatenate([queries, upstream[...]], axis=1), NN).astype(BF)


def attend_kernel(
    slots,
    asks,
    own,
    one,
    two,
    three,
    mixed,
    dquery,
    own_grads,
    one_grads,
    two_grads,
    three_grads,
):
    rows = asks.shape[0]
    width = asks.shape[1] // 2
    score_scale = 1.0 / math.sqrt(HDIM)
    split_heads, join_heads = head_splitter(width)

    def one_block(block, carry):
        here = pl.ds(pl.multiple_of(block * BLOCK, BLOCK), BLOCK)
        places = [here] + [
            pl.ds(pl.multiple_of(slots[which, block] * BLOCK, BLOCK), BLOCK)
            for which in FETCH_ORDER
        ]
        pairs = [source[place, :] for source, place in zip((own, one, two, three), places)]
        keys = jnp.concatenate([pair[:, :width] for pair in pairs], axis=0)
        values = jnp.concatenate([pair[:, width:] for pair in pairs], axis=0)
        query = split_heads(asks[here, :width])
        cotangent = split_heads(asks[here, width:])
        scores = mm(query, keys, NT) * score_scale
        peak = jnp.max(scores, axis=-1, keepdims=True)
        raised = jnp.exp(scores - peak)
        softmax = raised * (1.0 / jnp.sum(raised, axis=-1, keepdims=True))
        weights_low = softmax.astype(BF)
        mixed[here, :] = join_heads(mm(weights_low, values, NN)).astype(BF)
        dprobs = mm(cotangent, values, NT)
        row_delta = jnp.sum(softmax * dprobs, axis=-1, keepdims=True)
        dscores = (softmax * (dprobs - row_delta) * score_scale).astype(BF)
        dquery[here, :] = join_heads(mm(dscores, keys, NN)).astype(BF)
        dkeys = mm(dscores, query, TN)
        dvalues = mm(weights_low, cotangent, TN)
        targets = (own_grads, one_grads, two_grads, three_grads)
        for which, target in enumerate(targets):
            part = slice(which * BLOCK, (which + 1) * BLOCK)
            target[places[which], :width] = dkeys[part].astype(target.dtype)
            target[places[which], width:] = dvalues[part].astype(target.dtype)
        return carry

    lax.fori_loop(0, rows // BLOCK, one_block, 0)


def restore_kernel(mixed, order_row, mixed_nodes):
    rows = mixed.shape[0]
    node = lax.broadcasted_iota(jnp.int32, (rows, rows), 0)
    mixed_nodes[...] = mm(ones_where(node, order_row[...]), mixed[...], NN).astype(BF)


def query_kernel(features, order_row, dquery, dquery_nodes, weight_part):
    rows = dquery.shape[0]
    node = lax.broadcasted_iota(jnp.int32, (rows, rows), 0)
    dquery_nodes[...] = mm(ones_where(node, order_row[...]), dquery[...], NN).astype(BF)
    weight_part[...] = mm(features[...], dquery_nodes[...], TN).astype(BF)


def finish_kernel(
    place,
    features,
    weights,
    order_row,
    dquery_nodes,
    query_part,
    own,
    first,
    second,
    third,
    weight_part,
    keep,
    give,
    grad_nodes,
    chosen,
    own_held,
    others_held,
    arrived,
):
    rows, width = dquery_nodes.shape
    copies = [pltpu.make_async_copy(own, own_held, arrived.at[3])]
    for at, source in enumerate((first, second, third)):
        copies.append(pltpu.make_async_copy(source, others_held.at[at], arrived.at[at]))
    for copy in copies:
        copy.start()
    node = lax.broadcasted_iota(jnp.int32, (rows, rows), 0)
    restore = ones_where(node, order_row[...])
    for copy in copies:
        copy.wait()
    total = own_held[...]
    for at in range(3):
        total = total + others_held[at].astype(F32)
    pair_nodes = mm(restore, total.astype(BF), NN).astype(BF)
    weight_part[:, :width] = query_part[...]
    weight_part[:, width:] = mm(features[...], pair_nodes, TN).astype(BF)
    grad_nodes[:, :width] = dquery_nodes[...]
    grad_nodes[:, width:] = pair_nodes
    here = place[0]
    core = here % CORES
    chips = keep.shape[0] // BLOCK
    devices = chips * CORES
    share = rows // devices
    for flip, target in ((0, keep), (1, give)):
        own_row = here - core + (core + flip) % CORES
        for step in range(chips):
            at = pl.multiple_of((own_row + CORES * step) % devices * share, share)
            chosen[step * share : (step + 1) * share, :] = grad_nodes[pl.ds(at, share), :]
        target[...] = mm(chosen[...], weights[...], NT).astype(BF)


def local(features, node_order, partners, query_weight, key_weight, value_weight, upstream):
    width = query_weight.shape[1]
    depth = query_weight.shape[0]
    pair_weights = jnp.concatenate([key_weight, value_weight], axis=1)
    stacked = jnp.concatenate([query_weight, pair_weights], axis=1)
    rows = node_order.shape[0]
    blocks = rows // BLOCK
    slots = partners % blocks
    order_column = node_order.reshape(rows, 1)
    order_row = node_order.reshape(1, rows)
    levels = lax.axis_size("nodes").bit_length() - 1
    swap_bits = (0, levels - 2, levels - 1)
    params = pltpu.CompilerParams(vmem_limit_bytes=KERNEL_VMEM)
    place = lax.axis_index("heads").astype(jnp.int32).reshape(1)

    def shape(*dims, dtype=BF):
        return jax.ShapeDtypeStruct(dims, dtype)

    def swapped(blocks_for):
        return [
            from_partner(block, "nodes", swap_bits[which])
            for block, which in zip(blocks_for, FETCH_ORDER)
        ]

    arriving = lax.all_to_all(upstream, "heads", split_axis=1, concat_axis=0, tiled=True)
    pieces = gather_pieces(features)
    near, far, near_across, far_across = pieces
    near_pairs = pl.pallas_call(
        near_kernel,
        out_shape=shape(rows, 2 * width),
        in_specs=[SMEM] + [VMEM] * 4,
        out_specs=VMEM,
        compiler_params=params,
        name="project_near",
    )(place, near, near_across, pair_weights, order_column)
    far_across, arriving = lax.optimization_barrier((far_across, arriving))
    pairs = pl.pallas_call(
        far_kernel,
        out_shape=shape(rows, 2 * width),
        in_specs=[SMEM] + [VMEM] * 5,
        out_specs=VMEM,
        compiler_params=params,
        name="project_far",
    )(place, far, far_across, pair_weights, order_column, near_pairs)
    others = swapped([pairs] * 3)
    gathered, asks = pl.pallas_call(
        order_kernel,
        out_shape=(shape(rows, depth), shape(rows, 2 * width)),
        in_specs=[SMEM] + [ANY] * 4 + [VMEM] * 3,
        out_specs=(VMEM,) * 2,
        scratch_shapes=[pltpu.SemaphoreType.DMA((2 * CORES * CORES,))],
        compiler_params=params,
        name="order",
    )(place, near, far, near_across, far_across, query_weight, order_column, arriving)
    mixed, dquery, own_grads, *sent = pl.pallas_call(
        attend_kernel,
        out_shape=(
            shape(rows, width),
            shape(rows, width),
            shape(rows, 2 * width, dtype=F32),
            shape(rows, 2 * width),
            shape(rows, 2 * width),
            shape(rows, 2 * width),
        ),
        in_specs=[SMEM] + [VMEM] * 5,
        out_specs=(VMEM,) * 6,
        compiler_params=params,
        name="attend",
    )(slots, asks, pairs, *others)
    mixed_nodes = pl.pallas_call(
        restore_kernel,
        out_shape=shape(rows, width),
        in_specs=[VMEM] * 2,
        out_specs=VMEM,
        compiler_params=params,
        name="restore",
    )(mixed, order_row)
    returned = swapped(sent)
    mixed_nodes, *returned = lax.optimization_barrier((mixed_nodes, *returned))
    attended = lax.all_to_all(mixed_nodes, "heads", split_axis=0, concat_axis=1, tiled=True)
    dquery_nodes, query_part = pl.pallas_call(
        query_kernel,
        out_shape=(shape(rows, width), shape(depth, width)),
        in_specs=[VMEM] * 3,
        out_specs=(VMEM,) * 2,
        compiler_params=params,
        name="query_grads",
    )(gathered, order_row, dquery)
    weight_part, keep, give = pl.pallas_call(
        finish_kernel,
        out_shape=(
            shape(depth, 3 * width),
            shape(rows // CORES, depth),
            shape(rows // CORES, depth),
        ),
        in_specs=[SMEM] + [VMEM] * 5 + [ANY] * 4,
        out_specs=(VMEM,) * 3,
        scratch_shapes=[
            pltpu.VMEM((rows, 3 * width), BF),
            pltpu.VMEM((rows // CORES, 3 * width), BF),
            pltpu.VMEM((rows, 2 * width), F32),
            pltpu.VMEM((3, rows, 2 * width), BF),
            pltpu.SemaphoreType.DMA((4,)),
        ],
        compiler_params=params,
        name="finish",
    )(place, gathered, stacked, order_row, dquery_nodes, query_part, own_grads, *[returned[at] for at in RETURN_ORDER])
    weight_grads, feature_grad = summed(weight_part, keep, give)
    return (
        attended,
        feature_grad,
        weight_grads[:, :width],
        weight_grads[:, width : 2 * width],
        weight_grads[:, 2 * width :],
    )


def solution(mesh):
    return jax.shard_map(
        local,
        mesh=mesh,
        in_specs=(
            P(("nodes", "heads"), None),
            P("nodes"),
            P(None, "nodes"),
            P(None, "heads"),
            P(None, "heads"),
            P(None, "heads"),
            P(("nodes", "heads"), None),
        ),
        out_specs=(
            P(("nodes", "heads"), None),
            P(("nodes", "heads"), None),
            P(None, "heads"),
            P(None, "heads"),
            P(None, "heads"),
        ),
        check_vma=False,
    )
```

```python
import jax
import jax.numpy as jnp
from jax import lax
from jax.experimental import pallas as pl
from jax.experimental.pallas import tpu as pltpu
from jax.sharding import PartitionSpec as P

HDIM = 64
BLOCK = 128
CORES = 2
FETCH_ORDER = (1, 2, 0)
LOAD_ORDER = (0, 2, 1)
BF = jnp.bfloat16
F32 = jnp.float32
NN = (((1,), (0,)), ((), ()))
NT = (((1,), (1,)), ((), ()))
TN = (((0,), (0,)), ((), ()))
VMEM = pl.BlockSpec(memory_space=pltpu.VMEM)
SMEM = pl.BlockSpec(memory_space=pltpu.SMEM)
ANY = pl.BlockSpec(memory_space=pl.ANY)


def memory(mebibytes):
    return pltpu.CompilerParams(vmem_limit_bytes=mebibytes * 1024 * 1024)


def mm(a, b, dims):
    return lax.dot_general(a, b, dims, preferred_element_type=F32)


def from_partner(block, axis, bit):
    count = lax.axis_size(axis)
    route = []
    for low in range(count):
        high = low | 1 << bit
        if high != low and high < count:
            route += [(low, high), (high, low)]
    return lax.ppermute(block, axis, route)


def neighbours():
    count = lax.axis_size("heads")
    up = [(at, (at + CORES) % count) for at in range(count)]
    down = [((at + CORES) % count, at) for at in range(count)]
    across = [(at, at ^ 1) for at in range(count)]
    return up, down, across


def halves_of_nodes():
    count = lax.axis_size("nodes")
    return [list(range(count // 2)), list(range(count // 2, count))]


def exchange(block):
    return lax.all_to_all(block, "nodes", 0, 0, axis_index_groups=halves_of_nodes(), tiled=True)


def summed_here(spread):
    members = lax.axis_size("nodes") // 2
    share = jnp.sum(spread.reshape(members, -1, spread.shape[1]).astype(F32), axis=0)
    return share + from_partner(share, "nodes", members.bit_length() - 1)


def copies_of(share):
    members = lax.axis_size("nodes") // 2
    copies = jnp.broadcast_to(share.astype(BF)[None], (members,) + share.shape)
    return copies.reshape(-1, share.shape[1])


def gather_pieces(block):
    up, down, across = neighbours()
    half = block.shape[0] // 2
    from_low = lax.ppermute(block, "heads", up)
    from_high = lax.ppermute(block, "heads", down)
    far_low = lax.ppermute(from_low[:half], "heads", up)
    far_high = lax.ppermute(from_high[half:], "heads", down)
    near = jnp.concatenate([block, from_low, from_high], axis=0)
    far = jnp.concatenate([far_low, far_high], axis=0)
    near_across = lax.ppermute(near, "heads", across)
    return near, far, near_across, lax.ppermute(far, "heads", across)


def ones_where(rows_index, columns_index):
    return jnp.where(rows_index == columns_index, 1.0, 0.0).astype(BF)


def head_splitter(width):
    lane = lax.broadcasted_iota(jnp.int32, (BLOCK, width), 1) // HDIM
    heads = width // HDIM

    def split_heads(block):
        zero = jnp.zeros_like(block)
        return jnp.concatenate([jnp.where(lane == head, block, zero) for head in range(heads)], axis=0)

    def join_heads(stacked):
        joined = stacked[:BLOCK]
        for head in range(1, heads):
            joined = jnp.where(lane == head, stacked[head * BLOCK : (head + 1) * BLOCK], joined)
        return joined

    return split_heads, join_heads


def owners(place, flip):
    core = place % CORES
    return place - core + (core + flip) % CORES


def picks_of(order_column, bases, share):
    columns = lax.broadcasted_iota(jnp.int32, (order_column.shape[0], share), 1)
    return jnp.concatenate([ones_where(order_column - base, columns) for base in bases], axis=1)


def near_kernel(place, near, near_across, key_weight, value_weight, order_column, pairs):
    weights = jnp.concatenate([key_weight[...], value_weight[...]], axis=1)
    share = near.shape[0] // 3
    devices = order_column.shape[0] // share
    picks, projected = [], []
    for flip, piece in ((0, near), (1, near_across)):
        own = owners(place[0], flip)
        bases = [(own + step) % devices * share for step in (0, devices - CORES, CORES)]
        picks.append(picks_of(order_column[...], bases, share))
        projected.append(mm(piece[...], weights, NN).astype(BF))
    picked = jnp.concatenate(picks, axis=1)
    pairs[...] = mm(picked, jnp.concatenate(projected, axis=0), NN).astype(BF)


def far_kernel(
    place, far, far_across, key_weight, value_weight, order_column, near_pairs, pairs
):
    weights = jnp.concatenate([key_weight[...], value_weight[...]], axis=1)
    share = far.shape[0]
    devices = order_column.shape[0] // share
    bases = [(owners(place[0], flip) + devices // 2) % devices * share for flip in (0, 1)]
    both = jnp.concatenate([far[...], far_across[...]], axis=0)
    projected = mm(both, weights, NN).astype(BF)
    picked = mm(picks_of(order_column[...], bases, share), projected, NN).astype(BF)
    pairs[...] = near_pairs[...] + picked


def order_kernel(
    place, near, far, near_across, far_across, weights, order_column, upstream, gathered, asks, arrived
):
    rows = gathered.shape[0]
    share = far.shape[0]
    devices = rows // share
    copies = []
    for flip, close, distant in ((0, near, far), (1, near_across, far_across)):
        own = owners(place[0], flip)
        for step, source in (
            (0, close.at[pl.ds(0, share)]),
            (devices - CORES, close.at[pl.ds(share, share)]),
            (CORES, close.at[pl.ds(2 * share, share)]),
            (devices // 2, distant),
        ):
            at = pl.multiple_of((own + step) % devices * share, share)
            target = gathered.at[pl.ds(at, share)]
            copies.append(pltpu.make_async_copy(source, target, arrived.at[len(copies)]))
    for copy in copies:
        copy.start()
    node = lax.broadcasted_iota(jnp.int32, (rows, rows), 1)
    pick = ones_where(order_column[...], node)
    for copy in copies:
        copy.wait()
    queries = mm(gathered[...], weights[...], NN).astype(BF)
    asks[...] = mm(pick, jnp.concatenate([queries, upstream[...]], axis=1), NN).astype(BF)


def attend_kernel(
    slots,
    asks,
    own,
    one,
    two,
    three,
    mixed,
    dquery,
    own_grads,
    one_grads,
    two_grads,
    three_grads,
):
    rows = asks.shape[0]
    width = asks.shape[1] // 2
    score_scale = HDIM**-0.5
    split_heads, join_heads = head_splitter(width)

    def one_block(block, carry):
        here = pl.ds(pl.multiple_of(block * BLOCK, BLOCK), BLOCK)
        places = [here] + [
            pl.ds(pl.multiple_of(slots[which, block] * BLOCK, BLOCK), BLOCK)
            for which in FETCH_ORDER
        ]
        loads = dict(zip(LOAD_ORDER, (one, two, three)))
        sources = [own] + [loads[which] for which in FETCH_ORDER]
        pairs = [source[place, :] for source, place in zip(sources, places)]
        keys = jnp.concatenate([pair[:, :width] for pair in pairs], axis=0)
        values = jnp.concatenate([pair[:, width:] for pair in pairs], axis=0)
        query = split_heads(asks[here, :width] * score_scale)
        cotangent = split_heads(asks[here, width:])
        scores = mm(query, keys, NT)
        peak = jnp.max(scores, axis=-1, keepdims=True)
        raised = jnp.exp(scores - peak)
        softmax = raised * (1.0 / jnp.sum(raised, axis=-1, keepdims=True))
        weights_low = softmax.astype(BF)
        mixed[here, :] = join_heads(mm(weights_low, values, NN)).astype(BF)
        dprobs = mm(cotangent, values, NT)
        row_delta = jnp.sum(softmax * dprobs, axis=-1, keepdims=True)
        dscores = (softmax * (dprobs - row_delta)).astype(BF)
        dquery[here, :] = (join_heads(mm(dscores, keys, NN)) * score_scale).astype(BF)
        dkeys = mm(dscores, query, TN)
        dvalues = mm(weights_low, cotangent, TN)
        targets = (own_grads, one_grads, two_grads, three_grads)
        for which, target in enumerate(targets):
            part = slice(which * BLOCK, (which + 1) * BLOCK)
            target[places[which], :width] = dkeys[part].astype(target.dtype)
            target[places[which], width:] = dvalues[part].astype(target.dtype)
        return carry

    lax.fori_loop(0, rows // BLOCK, one_block, 0, unroll=4)


def restore_kernel(mixed, order_row, mixed_nodes):
    rows = mixed.shape[0]
    node = lax.broadcasted_iota(jnp.int32, (rows, rows), 0)
    mixed_nodes[...] = mm(ones_where(node, order_row[...]), mixed[...], NN).astype(BF)


def query_kernel(features, order_row, dquery, dquery_nodes, weight_part):
    rows = dquery.shape[0]
    node = lax.broadcasted_iota(jnp.int32, (rows, rows), 0)
    dquery_nodes[...] = mm(ones_where(node, order_row[...]), dquery[...], NN).astype(BF)
    weight_part[...] = mm(features[...], dquery_nodes[...], TN).astype(BF)


def finish_kernel(
    features,
    order_row,
    query_part,
    own,
    first,
    second,
    third,
    weight_part,
    pair_nodes,
    part_held,
    own_held,
    others_held,
    arrived,
):
    rows, pair_width = own.shape
    width = pair_width // 2
    early = pltpu.make_async_copy(query_part, weight_part.at[:, pl.ds(0, width)], arrived.at[4])
    early.start()
    copies = [pltpu.make_async_copy(own, own_held, arrived.at[3])]
    for at, source in enumerate((first, second, third)):
        copies.append(pltpu.make_async_copy(source, others_held.at[at], arrived.at[at]))
    for copy in copies:
        copy.start()
    node = lax.broadcasted_iota(jnp.int32, (rows, rows), 0)
    restore = ones_where(node, order_row[...])
    for copy in copies:
        copy.wait()
    total = own_held[...]
    for at in range(3):
        total = total + others_held[at].astype(F32)
    pair_nodes[...] = mm(restore, total.astype(BF), NN).astype(BF)
    part_held[...] = mm(features[...], pair_nodes[...], TN).astype(BF)
    last = pltpu.make_async_copy(part_held, weight_part.at[:, pl.ds(width, 2 * width)], arrived.at[0])
    last.start()
    last.wait()
    early.wait()


def features_kernel(
    place, dquery_nodes, pair_nodes, mixed_nodes, query_weight, key_weight, value_weight, keep, give, chosen
):
    rows, width = mixed_nodes.shape
    depth = query_weight.shape[0]
    weights = jnp.concatenate([query_weight[...], key_weight[...], value_weight[...]], axis=1)
    chips = keep.shape[0] // BLOCK
    devices = chips * CORES
    share = rows // devices
    for flip, target in ((0, keep), (1, give)):
        own = owners(place[0], flip)
        for step in range(chips):
            at = pl.multiple_of((own + CORES * step) % devices * share, share)
            to = slice(step * share, (step + 1) * share)
            chosen[to, :width] = dquery_nodes[pl.ds(at, share), :]
            chosen[to, width:] = pair_nodes[pl.ds(at, share), :]
            target[to, depth:] = mixed_nodes[pl.ds(at, share), :]
        target[:, :depth] = mm(chosen[...], weights, NT).astype(BF)


def total_of(*terms):
    return sum(term.astype(F32) for term in terms).astype(BF)


def far_rows_kernel(keep, got, to_high, to_low):
    all_width = keep.shape[1]
    depth = 2 * all_width - to_high.shape[1]
    half = to_high.shape[0]
    for at, target in ((4 * half, to_high), (5 * half, to_low)):
        part = slice(at, at + half)
        target[:, :depth] = total_of(keep[part, :depth], got[part, :depth])
        target[:, depth:all_width] = keep[part, depth:]
        target[:, all_width:] = got[part, depth:]


def near_rows_kernel(keep, got, from_low, from_high, to_high, to_low):
    all_width = keep.shape[1]
    both_width = from_low.shape[1]
    depth = 2 * all_width - both_width
    half = from_low.shape[0]
    for at, target, came, kept in ((2 * half, to_high, from_low, 0), (6 * half, to_low, from_high, half)):
        for step in (0, half):
            part = slice(at + step, at + step + half)
            to = slice(step, step + half)
            terms = [keep[part, :depth], got[part, :depth]]
            if step == kept:
                terms.append(came[:, :depth])
            target[to, :depth] = total_of(*terms)
            target[to, depth:all_width] = keep[part, depth:]
            target[to, all_width:both_width] = got[part, depth:]
        target[:half, both_width:] = came[:, depth:all_width]
        target[half:, both_width:] = came[:, all_width:]


def collect_kernel(place, keep, got, from_low, from_high, feature_grad, attended):
    rows, depth = feature_grad.shape
    width = keep.shape[1] - depth
    half = rows // 2
    devices = depth // width
    feature_grad[...] = total_of(
        keep[:rows, :depth], got[:rows, :depth], from_low[:, :depth], from_high[:, :depth]
    )
    for flip in (0, 1):
        own = owners(place[0], flip)
        start = depth + flip * width

        def columns(step):
            return pl.ds(pl.multiple_of((own + step) % devices * width, width), width)

        attended[:, columns(0)] = (keep, got)[flip][:rows, depth:]
        attended[:, columns(devices - CORES)] = from_low[:, start : start + width]
        attended[:, columns(CORES)] = from_high[:, start : start + width]
        part = slice(flip * half, (flip + 1) * half)
        attended[:half, columns(devices // 2)] = from_low[part, depth + 2 * width :]
        attended[half:, columns(devices // 2)] = from_high[part, depth + 2 * width :]


def local(features, node_order, partners, query_weight, key_weight, value_weight, upstream):
    width = query_weight.shape[1]
    depth = query_weight.shape[0]
    rows = node_order.shape[0]
    blocks = rows // BLOCK
    slots = partners % blocks
    order_column = node_order.reshape(rows, 1)
    order_row = node_order.reshape(1, rows)
    levels = lax.axis_size("nodes").bit_length() - 1
    swap_bits = (0, levels - 2, levels - 1)
    params = memory(12)
    up, down, across = neighbours()
    place = lax.axis_index("heads").astype(jnp.int32).reshape(1)

    def shape(*dims, dtype=BF):
        return jax.ShapeDtypeStruct(dims, dtype)

    def swapped(blocks_for):
        return [
            from_partner(block, "nodes", swap_bits[which])
            for block, which in zip(blocks_for, FETCH_ORDER)
        ]

    arriving = lax.all_to_all(upstream, "heads", split_axis=1, concat_axis=0, tiled=True)
    pieces = gather_pieces(features)
    near, far, near_across, far_across = pieces
    near_pairs = pl.pallas_call(
        near_kernel,
        out_shape=shape(rows, 2 * width),
        in_specs=[SMEM] + [VMEM] * 5,
        out_specs=VMEM,
        compiler_params=params,
        name="project_near",
    )(place, near, near_across, key_weight, value_weight, order_column)
    far_across, arriving = lax.optimization_barrier((far_across, arriving))
    pairs = pl.pallas_call(
        far_kernel,
        out_shape=shape(rows, 2 * width),
        in_specs=[SMEM] + [VMEM] * 6,
        out_specs=VMEM,
        compiler_params=params,
        name="project_far",
    )(place, far, far_across, key_weight, value_weight, order_column, near_pairs)
    others = [from_partner(pairs, "nodes", swap_bits[which]) for which in LOAD_ORDER]
    gathered, asks = pl.pallas_call(
        order_kernel,
        out_shape=(shape(rows, depth), shape(rows, 2 * width)),
        in_specs=[SMEM] + [ANY] * 4 + [VMEM] * 3,
        out_specs=(VMEM,) * 2,
        scratch_shapes=[pltpu.SemaphoreType.DMA((2 * CORES * CORES,))],
        compiler_params=params,
        name="order",
    )(place, near, far, near_across, far_across, query_weight, order_column, arriving)
    mixed, dquery, own_grads, *sent = pl.pallas_call(
        attend_kernel,
        out_shape=(
            shape(rows, width),
            shape(rows, width),
            shape(rows, 2 * width, dtype=F32),
            shape(rows, 2 * width),
            shape(rows, 2 * width),
            shape(rows, 2 * width),
        ),
        in_specs=[SMEM] + [VMEM] * 5,
        out_specs=(VMEM,) * 6,
        compiler_params=params,
        name="attend",
    )(slots, asks, pairs, *others)
    mixed_nodes = pl.pallas_call(
        restore_kernel,
        out_shape=shape(rows, width),
        in_specs=[VMEM] * 2,
        out_specs=VMEM,
        compiler_params=memory(8),
        name="restore",
    )(mixed, order_row)
    returned = swapped(sent)
    dquery_nodes, query_part = pl.pallas_call(
        query_kernel,
        out_shape=(shape(rows, width), shape(depth, width)),
        in_specs=[VMEM] * 3,
        out_specs=(VMEM,) * 2,
        compiler_params=params,
        name="query_grads",
    )(gathered, order_row, dquery)
    weight_part, pair_nodes = pl.pallas_call(
        finish_kernel,
        out_shape=(shape(depth, 3 * width), shape(rows, 2 * width)),
        in_specs=[VMEM] * 3 + [ANY] * 4,
        out_specs=(ANY, VMEM),
        scratch_shapes=[
            pltpu.VMEM((depth, 2 * width), BF),
            pltpu.VMEM((rows, 2 * width), F32),
            pltpu.VMEM((3, rows, 2 * width), BF),
            pltpu.SemaphoreType.DMA((5,)),
        ],
        compiler_params=params,
        name="finish",
    )(gathered, order_row, query_part, own_grads, *returned)
    spread = exchange(weight_part)

    share = rows // lax.axis_size("heads")
    full = depth + width
    keep, give = pl.pallas_call(
        features_kernel,
        out_shape=(shape(rows // CORES, full),) * 2,
        in_specs=[SMEM] + [VMEM] * 6,
        out_specs=(VMEM,) * 2,
        scratch_shapes=[pltpu.VMEM((rows // CORES, 3 * width), BF)],
        compiler_params=memory(6),
        name="features",
    )(place, dquery_nodes, pair_nodes, mixed_nodes, query_weight, key_weight, value_weight)
    got = lax.ppermute(give, "heads", across)
    to_high, to_low = pl.pallas_call(
        far_rows_kernel,
        out_shape=(shape(share // 2, full + width),) * 2,
        in_specs=[VMEM] * 2,
        out_specs=(VMEM,) * 2,
        compiler_params=memory(3),
        name="far_rows",
    )(keep, got)
    from_low = lax.ppermute(to_high, "heads", up)
    from_high = lax.ppermute(to_low, "heads", down)
    spread, from_low, from_high = lax.optimization_barrier((spread, from_low, from_high))
    weight_share = summed_here(spread)
    to_high, to_low = pl.pallas_call(
        near_rows_kernel,
        out_shape=(shape(share, full + 2 * width),) * 2,
        in_specs=[VMEM] * 4,
        out_specs=(VMEM,) * 2,
        compiler_params=memory(3),
        name="near_rows",
    )(keep, got, from_low, from_high)
    from_low = lax.ppermute(to_high, "heads", up)
    from_high = lax.ppermute(to_low, "heads", down)
    weight_grads = exchange(copies_of(weight_share))
    feature_grad, attended = pl.pallas_call(
        collect_kernel,
        out_shape=(shape(share, depth),) * 2,
        in_specs=[SMEM] + [VMEM] * 4,
        out_specs=(VMEM,) * 2,
        compiler_params=memory(3),
        name="collect",
    )(place, keep, got, from_low, from_high)
    query_grad, key_grad, value_grad = (
        weight_grads[:, at * width : (at + 1) * width].astype(F32) for at in range(3)
    )
    return attended, feature_grad, query_grad, key_grad, value_grad


def solution(mesh):
    return jax.shard_map(
        local,
        mesh=mesh,
        in_specs=(
            P(("nodes", "heads"), None),
            P("nodes"),
            P(None, "nodes"),
            P(None, "heads"),
            P(None, "heads"),
            P(None, "heads"),
            P(("nodes", "heads"), None),
        ),
        out_specs=(
            P(("nodes", "heads"), None),
            P(("nodes", "heads"), None),
            P(None, "heads"),
            P(None, "heads"),
            P(None, "heads"),
        ),
        check_vma=False,
    )
```

```python
import jax
import jax.numpy as jnp
from jax import lax
from jax.experimental import pallas as pl
from jax.experimental.pallas import tpu as pltpu
from jax.sharding import PartitionSpec as P

HDIM = 64
BLOCK = 128
CORES = 2
FETCH_ORDER = (1, 2, 0)
LOAD_ORDER = (0, 2, 1)
BF = jnp.bfloat16
F32 = jnp.float32
NN = (((1,), (0,)), ((), ()))
NT = (((1,), (1,)), ((), ()))
TN = (((0,), (0,)), ((), ()))
VMEM = pl.BlockSpec(memory_space=pltpu.VMEM)
SMEM = pl.BlockSpec(memory_space=pltpu.SMEM)
ANY = pl.BlockSpec(memory_space=pl.ANY)


def memory(mebibytes):
    return pltpu.CompilerParams(vmem_limit_bytes=mebibytes * 1024 * 1024)


def mm(a, b, dims):
    return lax.dot_general(a, b, dims, preferred_element_type=F32)


def from_partner(block, axis, bit):
    count = lax.axis_size(axis)
    route = []
    for low in range(count):
        high = low | 1 << bit
        if high != low and high < count:
            route += [(low, high), (high, low)]
    return lax.ppermute(block, axis, route)


def neighbours():
    count = lax.axis_size("heads")
    up = [(at, (at + CORES) % count) for at in range(count)]
    down = [((at + CORES) % count, at) for at in range(count)]
    across = [(at, at ^ 1) for at in range(count)]
    return up, down, across


def halves_of_nodes():
    count = lax.axis_size("nodes")
    return [list(range(count // 2)), list(range(count // 2, count))]


def exchange(block):
    return lax.all_to_all(block, "nodes", 0, 0, axis_index_groups=halves_of_nodes(), tiled=True)


def summed_here(spread):
    members = lax.axis_size("nodes") // 2
    share = jnp.sum(spread.reshape(members, -1, spread.shape[1]).astype(F32), axis=0)
    return share + from_partner(share, "nodes", members.bit_length() - 1)


def copies_of(share):
    members = lax.axis_size("nodes") // 2
    copies = jnp.broadcast_to(share.astype(BF)[None], (members,) + share.shape)
    return copies.reshape(-1, share.shape[1])


def gather_pieces(block, upstream):
    up, down, across = neighbours()
    half = block.shape[0] // 2
    from_low = lax.ppermute(block, "heads", up)
    from_high = lax.ppermute(block, "heads", down)
    from_low, upstream = lax.optimization_barrier((from_low, upstream))
    far_low = lax.ppermute(from_low[:half], "heads", up)
    far_high = lax.ppermute(from_high[half:], "heads", down)
    near = jnp.concatenate([block, from_low, from_high], axis=0)
    far = jnp.concatenate([far_low, far_high], axis=0)
    near_across = lax.ppermute(near, "heads", across)
    arriving = lax.all_to_all(upstream, "heads", split_axis=0, concat_axis=0, tiled=True)
    return near, far, near_across, lax.ppermute(far, "heads", across), arriving


def ones_where(rows_index, columns_index):
    return jnp.where(rows_index == columns_index, 1.0, 0.0).astype(BF)


def head_splitter(width):
    lane = lax.broadcasted_iota(jnp.int32, (BLOCK, width), 1) // HDIM
    heads = width // HDIM

    def split_heads(block):
        zero = jnp.zeros_like(block)
        return jnp.concatenate([jnp.where(lane == head, block, zero) for head in range(heads)], axis=0)

    def join_heads(stacked):
        joined = stacked[:BLOCK]
        for head in range(1, heads):
            joined = jnp.where(lane == head, stacked[head * BLOCK : (head + 1) * BLOCK], joined)
        return joined

    return split_heads, join_heads


def owners(place, flip):
    core = place % CORES
    return place - core + (core + flip) % CORES


def picks_of(order_column, bases, share):
    columns = lax.broadcasted_iota(jnp.int32, (order_column.shape[0], share), 1)
    return jnp.concatenate([ones_where(order_column - base, columns) for base in bases], axis=1)


def near_kernel(place, near, near_across, key_weight, value_weight, order_column, pairs):
    weights = jnp.concatenate([key_weight[...], value_weight[...]], axis=1)
    share = near.shape[0] // 3
    devices = order_column.shape[0] // share
    picks, projected = [], []
    for flip, piece in ((0, near), (1, near_across)):
        own = owners(place[0], flip)
        bases = [(own + step) % devices * share for step in (0, devices - CORES, CORES)]
        picks.append(picks_of(order_column[...], bases, share))
        projected.append(mm(piece[...], weights, NN).astype(BF))
    picked = jnp.concatenate(picks, axis=1)
    pairs[...] = mm(picked, jnp.concatenate(projected, axis=0), NN).astype(BF)


def far_kernel(
    place, far, far_across, key_weight, value_weight, order_column, near_pairs, pairs
):
    weights = jnp.concatenate([key_weight[...], value_weight[...]], axis=1)
    share = far.shape[0]
    devices = order_column.shape[0] // share
    bases = [(owners(place[0], flip) + devices // 2) % devices * share for flip in (0, 1)]
    both = jnp.concatenate([far[...], far_across[...]], axis=0)
    projected = mm(both, weights, NN).astype(BF)
    picked = mm(picks_of(order_column[...], bases, share), projected, NN).astype(BF)
    pairs[...] = near_pairs[...] + picked


def order_kernel(
    place, near, far, near_across, far_across, weights, order_column, upstream, gathered, asks, arrived
):
    rows = gathered.shape[0]
    share = far.shape[0]
    devices = rows // share
    copies = []
    for flip, close, distant in ((0, near, far), (1, near_across, far_across)):
        own = owners(place[0], flip)
        for step, source in (
            (0, close.at[pl.ds(0, share)]),
            (devices - CORES, close.at[pl.ds(share, share)]),
            (CORES, close.at[pl.ds(2 * share, share)]),
            (devices // 2, distant),
        ):
            at = pl.multiple_of((own + step) % devices * share, share)
            target = gathered.at[pl.ds(at, share)]
            copies.append(pltpu.make_async_copy(source, target, arrived.at[len(copies)]))
    for copy in copies:
        copy.start()
    node = lax.broadcasted_iota(jnp.int32, (rows, rows), 1)
    pick = ones_where(order_column[...], node)
    for copy in copies:
        copy.wait()
    queries = mm(gathered[...], weights[...], NN).astype(BF)
    asks[...] = mm(pick, jnp.concatenate([queries, upstream[...]], axis=1), NN).astype(BF)


def attend_kernel(
    slots,
    asks,
    own,
    one,
    two,
    three,
    mixed,
    dquery,
    own_grads,
    one_grads,
    two_grads,
    three_grads,
):
    rows = asks.shape[0]
    width = asks.shape[1] // 2
    score_scale = HDIM**-0.5
    split_heads, join_heads = head_splitter(width)

    def one_block(block, carry):
        here = pl.ds(pl.multiple_of(block * BLOCK, BLOCK), BLOCK)
        places = [here] + [
            pl.ds(pl.multiple_of(slots[which, block] * BLOCK, BLOCK), BLOCK)
            for which in FETCH_ORDER
        ]
        loads = dict(zip(LOAD_ORDER, (one, two, three)))
        sources = [own] + [loads[which] for which in FETCH_ORDER]
        pairs = [source[place, :] for source, place in zip(sources, places)]
        keys = jnp.concatenate([pair[:, :width] for pair in pairs], axis=0)
        values = jnp.concatenate([pair[:, width:] for pair in pairs], axis=0)
        query = split_heads(asks[here, :width] * score_scale)
        cotangent = split_heads(asks[here, width:])
        scores = mm(query, keys, NT)
        peak = jnp.max(scores, axis=-1, keepdims=True)
        raised = jnp.exp(scores - peak)
        softmax = raised * (1.0 / jnp.sum(raised, axis=-1, keepdims=True))
        weights_low = softmax.astype(BF)
        mixed[here, :] = join_heads(mm(weights_low, values, NN)).astype(BF)
        dprobs = mm(cotangent, values, NT)
        row_delta = jnp.sum(softmax * dprobs, axis=-1, keepdims=True)
        dscores = (softmax * (dprobs - row_delta)).astype(BF)
        dquery[here, :] = (join_heads(mm(dscores, keys, NN)) * score_scale).astype(BF)
        dkeys = mm(dscores, query, TN)
        dvalues = mm(weights_low, cotangent, TN)
        targets = (own_grads, one_grads, two_grads, three_grads)
        for which, target in enumerate(targets):
            part = slice(which * BLOCK, (which + 1) * BLOCK)
            target[places[which], :width] = dkeys[part].astype(target.dtype)
            target[places[which], width:] = dvalues[part].astype(target.dtype)
        return carry

    lax.fori_loop(0, rows // BLOCK, one_block, 0, unroll=4)


def restore_kernel(mixed, order_row, mixed_nodes):
    rows = mixed.shape[0]
    node = lax.broadcasted_iota(jnp.int32, (rows, rows), 0)
    mixed_nodes[...] = mm(ones_where(node, order_row[...]), mixed[...], NN).astype(BF)


def query_kernel(features, order_row, dquery, dquery_nodes, weight_part):
    rows = dquery.shape[0]
    node = lax.broadcasted_iota(jnp.int32, (rows, rows), 0)
    dquery_nodes[...] = mm(ones_where(node, order_row[...]), dquery[...], NN).astype(BF)
    weight_part[...] = mm(features[...], dquery_nodes[...], TN).astype(BF)


def finish_kernel(
    features,
    order_row,
    query_part,
    own,
    first,
    second,
    third,
    weight_part,
    pair_nodes,
    part_held,
    own_held,
    others_held,
    arrived,
):
    rows, pair_width = own.shape
    width = pair_width // 2
    early = pltpu.make_async_copy(query_part, weight_part.at[:, pl.ds(0, width)], arrived.at[4])
    early.start()
    copies = [pltpu.make_async_copy(own, own_held, arrived.at[3])]
    for at, source in enumerate((first, second, third)):
        copies.append(pltpu.make_async_copy(source, others_held.at[at], arrived.at[at]))
    for copy in copies:
        copy.start()
    node = lax.broadcasted_iota(jnp.int32, (rows, rows), 0)
    restore = ones_where(node, order_row[...])
    for copy in copies:
        copy.wait()
    total = own_held[...]
    for at in range(3):
        total = total + others_held[at].astype(F32)
    pair_nodes[...] = mm(restore, total.astype(BF), NN).astype(BF)
    part_held[...] = mm(features[...], pair_nodes[...], TN).astype(BF)
    last = pltpu.make_async_copy(part_held, weight_part.at[:, pl.ds(width, 2 * width)], arrived.at[0])
    last.start()
    last.wait()
    early.wait()


def features_kernel(
    place, dquery_nodes, pair_nodes, mixed_nodes, query_weight, key_weight, value_weight, keep, give, chosen
):
    rows, width = mixed_nodes.shape
    depth = query_weight.shape[0]
    weights = jnp.concatenate([query_weight[...], key_weight[...], value_weight[...]], axis=1)
    chips = keep.shape[0] // BLOCK
    devices = chips * CORES
    share = rows // devices
    for flip, target in ((0, keep), (1, give)):
        own = owners(place[0], flip)
        for step in range(chips):
            at = pl.multiple_of((own + CORES * step) % devices * share, share)
            to = slice(step * share, (step + 1) * share)
            chosen[to, :width] = dquery_nodes[pl.ds(at, share), :]
            chosen[to, width:] = pair_nodes[pl.ds(at, share), :]
            target[to, depth:] = mixed_nodes[pl.ds(at, share), :]
        target[:, :depth] = mm(chosen[...], weights, NT).astype(BF)


def total_of(*terms):
    return sum(term.astype(F32) for term in terms).astype(BF)


def far_rows_kernel(keep, got, to_high, to_low):
    all_width = keep.shape[1]
    depth = 2 * all_width - to_high.shape[1]
    half = to_high.shape[0]
    for at, target in ((4 * half, to_high), (5 * half, to_low)):
        part = slice(at, at + half)
        target[:, :depth] = total_of(keep[part, :depth], got[part, :depth])
        target[:, depth:all_width] = keep[part, depth:]
        target[:, all_width:] = got[part, depth:]


def near_rows_kernel(keep, got, from_low, from_high, to_high, to_low):
    all_width = keep.shape[1]
    both_width = from_low.shape[1]
    depth = 2 * all_width - both_width
    half = from_low.shape[0]
    for at, target, came, kept in ((2 * half, to_high, from_low, 0), (6 * half, to_low, from_high, half)):
        for step in (0, half):
            part = slice(at + step, at + step + half)
            to = slice(step, step + half)
            terms = [keep[part, :depth], got[part, :depth]]
            if step == kept:
                terms.append(came[:, :depth])
            target[to, :depth] = total_of(*terms)
            target[to, depth:all_width] = keep[part, depth:]
            target[to, all_width:both_width] = got[part, depth:]
        target[:half, both_width:] = came[:, depth:all_width]
        target[half:, both_width:] = came[:, all_width:]


def collect_kernel(place, keep, got, from_low, from_high, feature_grad, attended):
    rows, depth = feature_grad.shape
    width = keep.shape[1] - depth
    half = rows // 2
    devices = depth // width
    feature_grad[...] = total_of(
        keep[:rows, :depth], got[:rows, :depth], from_low[:, :depth], from_high[:, :depth]
    )
    for flip in (0, 1):
        own = owners(place[0], flip)
        start = depth + flip * width

        def columns(step):
            return pl.ds(pl.multiple_of((own + step) % devices * width, width), width)

        attended[:, columns(0)] = (keep, got)[flip][:rows, depth:]
        attended[:, columns(devices - CORES)] = from_low[:, start : start + width]
        attended[:, columns(CORES)] = from_high[:, start : start + width]
        part = slice(flip * half, (flip + 1) * half)
        attended[:half, columns(devices // 2)] = from_low[part, depth + 2 * width :]
        attended[half:, columns(devices // 2)] = from_high[part, depth + 2 * width :]


def widen_kernel(whole, *parts):
    width = parts[0].shape[1]
    for at, part in enumerate(parts):
        part[...] = whole[:, at * width : (at + 1) * width].astype(F32)


def local(features, node_order, partners, query_weight, key_weight, value_weight, upstream):
    width = query_weight.shape[1]
    depth = query_weight.shape[0]
    rows = node_order.shape[0]
    blocks = rows // BLOCK
    slots = partners % blocks
    order_column = node_order.reshape(rows, 1)
    order_row = node_order.reshape(1, rows)
    levels = lax.axis_size("nodes").bit_length() - 1
    swap_bits = (0, levels - 2, levels - 1)
    params = memory(12)
    up, down, across = neighbours()
    place = lax.axis_index("heads").astype(jnp.int32).reshape(1)

    def shape(*dims, dtype=BF):
        return jax.ShapeDtypeStruct(dims, dtype)

    def swapped(blocks_for):
        return [
            from_partner(block, "nodes", swap_bits[which])
            for block, which in zip(blocks_for, FETCH_ORDER)
        ]

    by_heads = upstream.reshape(-1, depth // width, width).swapaxes(0, 1).reshape(rows, width)
    near, far, near_across, far_across, arriving = gather_pieces(features, by_heads)
    near_pairs = pl.pallas_call(
        near_kernel,
        out_shape=shape(rows, 2 * width),
        in_specs=[SMEM] + [VMEM] * 5,
        out_specs=VMEM,
        compiler_params=params,
        name="project_near",
    )(place, near, near_across, key_weight, value_weight, order_column)
    far_across, arriving = lax.optimization_barrier((far_across, arriving))
    pairs = pl.pallas_call(
        far_kernel,
        out_shape=shape(rows, 2 * width),
        in_specs=[SMEM] + [VMEM] * 6,
        out_specs=VMEM,
        compiler_params=params,
        name="project_far",
    )(place, far, far_across, key_weight, value_weight, order_column, near_pairs)
    others = [from_partner(pairs, "nodes", swap_bits[which]) for which in LOAD_ORDER]
    gathered, asks = pl.pallas_call(
        order_kernel,
        out_shape=(shape(rows, depth), shape(rows, 2 * width)),
        in_specs=[SMEM] + [ANY] * 4 + [VMEM] * 3,
        out_specs=(VMEM,) * 2,
        scratch_shapes=[pltpu.SemaphoreType.DMA((2 * CORES * CORES,))],
        compiler_params=params,
        name="order",
    )(place, near, far, near_across, far_across, query_weight, order_column, arriving)
    mixed, dquery, own_grads, *sent = pl.pallas_call(
        attend_kernel,
        out_shape=(
            shape(rows, width),
            shape(rows, width),
            shape(rows, 2 * width, dtype=F32),
            shape(rows, 2 * width),
            shape(rows, 2 * width),
            shape(rows, 2 * width),
        ),
        in_specs=[SMEM] + [VMEM] * 5,
        out_specs=(VMEM,) * 6,
        compiler_params=params,
        name="attend",
    )(slots, asks, pairs, *others)
    mixed_nodes = pl.pallas_call(
        restore_kernel,
        out_shape=shape(rows, width),
        in_specs=[VMEM] * 2,
        out_specs=VMEM,
        compiler_params=memory(8),
        name="restore",
    )(mixed, order_row)
    returned = swapped(sent)
    dquery_nodes, query_part = pl.pallas_call(
        query_kernel,
        out_shape=(shape(rows, width), shape(depth, width)),
        in_specs=[VMEM] * 3,
        out_specs=(VMEM,) * 2,
        compiler_params=params,
        name="query_grads",
    )(gathered, order_row, dquery)
    weight_part, pair_nodes = pl.pallas_call(
        finish_kernel,
        out_shape=(shape(depth, 3 * width), shape(rows, 2 * width)),
        in_specs=[VMEM] * 3 + [ANY] * 4,
        out_specs=(ANY, VMEM),
        scratch_shapes=[
            pltpu.VMEM((depth, 2 * width), BF),
            pltpu.VMEM((rows, 2 * width), F32),
            pltpu.VMEM((3, rows, 2 * width), BF),
            pltpu.SemaphoreType.DMA((5,)),
        ],
        compiler_params=params,
        name="finish",
    )(gathered, order_row, query_part, own_grads, *returned)
    spread = exchange(weight_part)

    share = rows // lax.axis_size("heads")
    full = depth + width
    keep, give = pl.pallas_call(
        features_kernel,
        out_shape=(shape(rows // CORES, full),) * 2,
        in_specs=[SMEM] + [VMEM] * 6,
        out_specs=(VMEM,) * 2,
        scratch_shapes=[pltpu.VMEM((rows // CORES, 3 * width), BF)],
        compiler_params=memory(6),
        name="features",
    )(place, dquery_nodes, pair_nodes, mixed_nodes, query_weight, key_weight, value_weight)
    got = lax.ppermute(give, "heads", across)
    to_high, to_low = pl.pallas_call(
        far_rows_kernel,
        out_shape=(shape(share // 2, full + width),) * 2,
        in_specs=[VMEM] * 2,
        out_specs=(VMEM,) * 2,
        compiler_params=memory(3),
        name="far_rows",
    )(keep, got)
    from_low = lax.ppermute(to_high, "heads", up)
    from_high = lax.ppermute(to_low, "heads", down)
    spread, from_low, from_high = lax.optimization_barrier((spread, from_low, from_high))
    weight_share = summed_here(spread)
    to_high, to_low = pl.pallas_call(
        near_rows_kernel,
        out_shape=(shape(share, full + 2 * width),) * 2,
        in_specs=[VMEM] * 4,
        out_specs=(VMEM,) * 2,
        compiler_params=memory(3),
        name="near_rows",
    )(keep, got, from_low, from_high)
    from_low = lax.ppermute(to_high, "heads", up)
    from_high = lax.ppermute(to_low, "heads", down)
    weight_grads = exchange(copies_of(weight_share))
    feature_grad, attended = pl.pallas_call(
        collect_kernel,
        out_shape=(shape(share, depth),) * 2,
        in_specs=[SMEM] + [VMEM] * 4,
        out_specs=(VMEM,) * 2,
        compiler_params=memory(3),
        name="collect",
    )(place, keep, got, from_low, from_high)
    piece = depth // 4
    query_grad, key_grad, value_grad = pl.pallas_call(
        widen_kernel,
        grid=(4,),
        out_shape=(shape(depth, width, dtype=F32),) * 3,
        in_specs=[pl.BlockSpec((piece, 3 * width), lambda at: (at, 0))],
        out_specs=(pl.BlockSpec((piece, width), lambda at: (at, 0)),) * 3,
        compiler_params=memory(3),
        name="widen",
    )(weight_grads)
    return attended, feature_grad, query_grad, key_grad, value_grad


def solution(mesh):
    return jax.shard_map(
        local,
        mesh=mesh,
        in_specs=(
            P(("nodes", "heads"), None),
            P("nodes"),
            P(None, "nodes"),
            P(None, "heads"),
            P(None, "heads"),
            P(None, "heads"),
            P(("nodes", "heads"), None),
        ),
        out_specs=(
            P(("nodes", "heads"), None),
            P(("nodes", "heads"), None),
            P(None, "heads"),
            P(None, "heads"),
            P(None, "heads"),
        ),
        check_vma=False,
    )
```

```python
import jax
import jax.numpy as jnp
from jax import lax
from jax.experimental import pallas as pl
from jax.experimental.pallas import tpu as pltpu
from jax.sharding import PartitionSpec as P

HDIM = 64
BLOCK = 128
CORES = 2
FETCH_ORDER = (1, 2, 0)
LOAD_ORDER = (0, 2, 1)
BF = jnp.bfloat16
F32 = jnp.float32
NN = (((1,), (0,)), ((), ()))
NT = (((1,), (1,)), ((), ()))
TN = (((0,), (0,)), ((), ()))
VMEM = pl.BlockSpec(memory_space=pltpu.VMEM)
SMEM = pl.BlockSpec(memory_space=pltpu.SMEM)
ANY = pl.BlockSpec(memory_space=pl.ANY)


def memory(mebibytes):
    return pltpu.CompilerParams(vmem_limit_bytes=mebibytes * 1024 * 1024)


def mm(a, b, dims):
    return lax.dot_general(a, b, dims, preferred_element_type=F32)


def from_partner(block, axis, bit):
    count = lax.axis_size(axis)
    route = []
    for low in range(count):
        high = low | 1 << bit
        if high != low and high < count:
            route += [(low, high), (high, low)]
    return lax.ppermute(block, axis, route)


def neighbours():
    count = lax.axis_size("heads")
    up = [(at, (at + CORES) % count) for at in range(count)]
    down = [((at + CORES) % count, at) for at in range(count)]
    across = [(at, at ^ 1) for at in range(count)]
    return up, down, across


def halves_of_nodes():
    count = lax.axis_size("nodes")
    return [list(range(count // 2)), list(range(count // 2, count))]


def exchange(block):
    return lax.all_to_all(block, "nodes", 0, 0, axis_index_groups=halves_of_nodes(), tiled=True)


def summed_here(spread):
    members = lax.axis_size("nodes") // 2
    share = jnp.sum(spread.reshape(members, -1, spread.shape[1]).astype(F32), axis=0)
    return share + from_partner(share, "nodes", members.bit_length() - 1)


def copies_of(share):
    members = lax.axis_size("nodes") // 2
    copies = jnp.broadcast_to(share.astype(BF)[None], (members,) + share.shape)
    return copies.reshape(-1, share.shape[1])


def gather_pieces(block, upstream):
    up, down, across = neighbours()
    half = block.shape[0] // 2
    from_low = lax.ppermute(block, "heads", up)
    from_high = lax.ppermute(block, "heads", down)
    from_low, upstream = lax.optimization_barrier((from_low, upstream))
    far_low = lax.ppermute(from_low[:half], "heads", up)
    far_high = lax.ppermute(from_high[half:], "heads", down)
    near = jnp.concatenate([block, from_low, from_high], axis=0)
    far = jnp.concatenate([far_low, far_high], axis=0)
    near_across = lax.ppermute(near, "heads", across)
    arriving = lax.all_to_all(upstream, "heads", split_axis=0, concat_axis=0, tiled=True)
    return near, far, near_across, lax.ppermute(far, "heads", across), arriving


def ones_where(rows_index, columns_index):
    return jnp.where(rows_index == columns_index, 1.0, 0.0).astype(BF)


def head_splitter(width):
    lane = lax.broadcasted_iota(jnp.int32, (BLOCK, width), 1) // HDIM
    heads = width // HDIM

    def split_heads(block):
        zero = jnp.zeros_like(block)
        return jnp.concatenate([jnp.where(lane == head, block, zero) for head in range(heads)], axis=0)

    def join_heads(stacked):
        joined = stacked[:BLOCK]
        for head in range(1, heads):
            joined = jnp.where(lane == head, stacked[head * BLOCK : (head + 1) * BLOCK], joined)
        return joined

    return split_heads, join_heads


def owners(place, flip):
    core = place % CORES
    return place - core + (core + flip) % CORES


def picks_of(order_column, bases, share):
    columns = lax.broadcasted_iota(jnp.int32, (order_column.shape[0], share), 1)
    return jnp.concatenate([ones_where(order_column - base, columns) for base in bases], axis=1)


def near_kernel(place, near, near_across, key_weight, value_weight, order_column, pairs):
    weights = jnp.concatenate([key_weight[...], value_weight[...]], axis=1)
    share = near.shape[0] // 3
    devices = order_column.shape[0] // share
    picks, projected = [], []
    for flip, piece in ((0, near), (1, near_across)):
        own = owners(place[0], flip)
        bases = [(own + step) % devices * share for step in (0, devices - CORES, CORES)]
        picks.append(picks_of(order_column[...], bases, share))
        projected.append(mm(piece[...], weights, NN).astype(BF))
    picked = jnp.concatenate(picks, axis=1)
    pairs[...] = mm(picked, jnp.concatenate(projected, axis=0), NN).astype(BF)


def far_kernel(
    place, far, far_across, key_weight, value_weight, order_column, near_pairs, pairs
):
    weights = jnp.concatenate([key_weight[...], value_weight[...]], axis=1)
    share = far.shape[0]
    devices = order_column.shape[0] // share
    bases = [(owners(place[0], flip) + devices // 2) % devices * share for flip in (0, 1)]
    both = jnp.concatenate([far[...], far_across[...]], axis=0)
    projected = mm(both, weights, NN).astype(BF)
    picked = mm(picks_of(order_column[...], bases, share), projected, NN).astype(BF)
    pairs[...] = near_pairs[...] + picked


def order_kernel(
    place, near, far, near_across, far_across, weights, order_column, upstream, gathered, asks, arrived
):
    rows = gathered.shape[0]
    share = far.shape[0]
    devices = rows // share
    copies = []
    for flip, close, distant in ((0, near, far), (1, near_across, far_across)):
        own = owners(place[0], flip)
        for step, source in (
            (0, close.at[pl.ds(0, share)]),
            (devices - CORES, close.at[pl.ds(share, share)]),
            (CORES, close.at[pl.ds(2 * share, share)]),
            (devices // 2, distant),
        ):
            at = pl.multiple_of((own + step) % devices * share, share)
            target = gathered.at[pl.ds(at, share)]
            copies.append(pltpu.make_async_copy(source, target, arrived.at[len(copies)]))
    for copy in copies:
        copy.start()
    node = lax.broadcasted_iota(jnp.int32, (rows, rows), 1)
    pick = ones_where(order_column[...], node)
    for copy in copies:
        copy.wait()
    queries = mm(gathered[...], weights[...], NN).astype(BF)
    asks[...] = mm(pick, jnp.concatenate([queries, upstream[...]], axis=1), NN).astype(BF)


def attend_kernel(
    slots,
    asks,
    own,
    one,
    two,
    three,
    mixed,
    dquery,
    own_grads,
    one_grads,
    two_grads,
    three_grads,
):
    rows = asks.shape[0]
    width = asks.shape[1] // 2
    score_scale = HDIM**-0.5
    split_heads, join_heads = head_splitter(width)

    def one_block(block, carry):
        here = pl.ds(pl.multiple_of(block * BLOCK, BLOCK), BLOCK)
        places = [here] + [
            pl.ds(pl.multiple_of(slots[which, block] * BLOCK, BLOCK), BLOCK)
            for which in FETCH_ORDER
        ]
        loads = dict(zip(LOAD_ORDER, (one, two, three)))
        sources = [own] + [loads[which] for which in FETCH_ORDER]
        pairs = [source[place, :] for source, place in zip(sources, places)]
        keys = jnp.concatenate([pair[:, :width] for pair in pairs], axis=0)
        values = jnp.concatenate([pair[:, width:] for pair in pairs], axis=0)
        query = split_heads(asks[here, :width] * score_scale)
        cotangent = split_heads(asks[here, width:])
        scores = mm(query, keys, NT)
        peak = jnp.max(scores, axis=-1, keepdims=True)
        raised = jnp.exp(scores - peak)
        softmax = raised * (1.0 / jnp.sum(raised, axis=-1, keepdims=True))
        weights_low = softmax.astype(BF)
        mixed[here, :] = join_heads(mm(weights_low, values, NN)).astype(BF)
        dprobs = mm(cotangent, values, NT)
        row_delta = jnp.sum(softmax * dprobs, axis=-1, keepdims=True)
        dscores = (softmax * (dprobs - row_delta)).astype(BF)
        dquery[here, :] = (join_heads(mm(dscores, keys, NN)) * score_scale).astype(BF)
        dkeys = mm(dscores, query, TN)
        dvalues = mm(weights_low, cotangent, TN)
        targets = (own_grads, one_grads, two_grads, three_grads)
        for which, target in enumerate(targets):
            part = slice(which * BLOCK, (which + 1) * BLOCK)
            target[places[which], :width] = dkeys[part].astype(target.dtype)
            target[places[which], width:] = dvalues[part].astype(target.dtype)
        return carry

    lax.fori_loop(0, rows // BLOCK, one_block, 0, unroll=8)


def restore_kernel(mixed, order_row, mixed_nodes):
    rows = mixed.shape[0]
    node = lax.broadcasted_iota(jnp.int32, (rows, rows), 0)
    mixed_nodes[...] = mm(ones_where(node, order_row[...]), mixed[...], NN).astype(BF)


def query_kernel(features, order_row, dquery, dquery_nodes, weight_part):
    rows = dquery.shape[0]
    node = lax.broadcasted_iota(jnp.int32, (rows, rows), 0)
    dquery_nodes[...] = mm(ones_where(node, order_row[...]), dquery[...], NN).astype(BF)
    weight_part[...] = mm(features[...], dquery_nodes[...], TN).astype(BF)


def finish_kernel(
    features,
    order_row,
    query_part,
    own,
    first,
    second,
    third,
    weight_part,
    pair_nodes,
    part_held,
    arrived,
):
    rows, pair_width = own.shape
    width = pair_width // 2
    early = pltpu.make_async_copy(query_part, weight_part.at[:, pl.ds(0, width)], arrived.at[1])
    early.start()
    node = lax.broadcasted_iota(jnp.int32, (rows, rows), 0)
    restore = ones_where(node, order_row[...])
    total = own[...]
    for other in (first, second, third):
        total = total + other[...].astype(F32)
    pair_nodes[...] = mm(restore, total.astype(BF), NN).astype(BF)
    part_held[...] = mm(features[...], pair_nodes[...], TN).astype(BF)
    last = pltpu.make_async_copy(part_held, weight_part.at[:, pl.ds(width, 2 * width)], arrived.at[0])
    last.start()
    last.wait()
    early.wait()


def features_kernel(
    place, dquery_nodes, pair_nodes, mixed_nodes, query_weight, key_weight, value_weight, keep, give, chosen
):
    rows, width = mixed_nodes.shape
    depth = query_weight.shape[0]
    weights = jnp.concatenate([query_weight[...], key_weight[...], value_weight[...]], axis=1)
    chips = keep.shape[0] // BLOCK
    devices = chips * CORES
    share = rows // devices
    for flip, target in ((0, keep), (1, give)):
        own = owners(place[0], flip)
        for step in range(chips):
            at = pl.multiple_of((own + CORES * step) % devices * share, share)
            to = slice(step * share, (step + 1) * share)
            chosen[to, :width] = dquery_nodes[pl.ds(at, share), :]
            chosen[to, width:] = pair_nodes[pl.ds(at, share), :]
            target[to, depth:] = mixed_nodes[pl.ds(at, share), :]
        target[:, :depth] = mm(chosen[...], weights, NT).astype(BF)


def total_of(*terms):
    return sum(term.astype(F32) for term in terms).astype(BF)


def far_rows_kernel(keep, got, to_high, to_low):
    all_width = keep.shape[1]
    depth = 2 * all_width - to_high.shape[1]
    half = to_high.shape[0]
    for at, target in ((4 * half, to_high), (5 * half, to_low)):
        part = slice(at, at + half)
        target[:, :depth] = total_of(keep[part, :depth], got[part, :depth])
        target[:, depth:all_width] = keep[part, depth:]
        target[:, all_width:] = got[part, depth:]


def near_rows_kernel(keep, got, from_low, from_high, to_high, to_low):
    all_width = keep.shape[1]
    both_width = from_low.shape[1]
    depth = 2 * all_width - both_width
    half = from_low.shape[0]
    for at, target, came, kept in ((2 * half, to_high, from_low, 0), (6 * half, to_low, from_high, half)):
        for step in (0, half):
            part = slice(at + step, at + step + half)
            to = slice(step, step + half)
            terms = [keep[part, :depth], got[part, :depth]]
            if step == kept:
                terms.append(came[:, :depth])
            target[to, :depth] = total_of(*terms)
            target[to, depth:all_width] = keep[part, depth:]
            target[to, all_width:both_width] = got[part, depth:]
        target[:half, both_width:] = came[:, depth:all_width]
        target[half:, both_width:] = came[:, all_width:]


def collect_kernel(place, keep, got, from_low, from_high, feature_grad, attended):
    rows, depth = feature_grad.shape
    width = keep.shape[1] - depth
    half = rows // 2
    devices = depth // width
    feature_grad[...] = total_of(
        keep[:rows, :depth], got[:rows, :depth], from_low[:, :depth], from_high[:, :depth]
    )
    for flip in (0, 1):
        own = owners(place[0], flip)
        start = depth + flip * width

        def columns(step):
            return pl.ds(pl.multiple_of((own + step) % devices * width, width), width)

        attended[:, columns(0)] = (keep, got)[flip][:rows, depth:]
        attended[:, columns(devices - CORES)] = from_low[:, start : start + width]
        attended[:, columns(CORES)] = from_high[:, start : start + width]
        part = slice(flip * half, (flip + 1) * half)
        attended[:half, columns(devices // 2)] = from_low[part, depth + 2 * width :]
        attended[half:, columns(devices // 2)] = from_high[part, depth + 2 * width :]


def widen_kernel(whole, *parts):
    width = parts[0].shape[1]
    for at, part in enumerate(parts):
        part[...] = whole[:, at * width : (at + 1) * width].astype(F32)


def local(features, node_order, partners, query_weight, key_weight, value_weight, upstream):
    width = query_weight.shape[1]
    depth = query_weight.shape[0]
    rows = node_order.shape[0]
    blocks = rows // BLOCK
    slots = partners % blocks
    order_column = node_order.reshape(rows, 1)
    order_row = node_order.reshape(1, rows)
    levels = lax.axis_size("nodes").bit_length() - 1
    swap_bits = (0, levels - 2, levels - 1)
    params = memory(12)
    up, down, across = neighbours()
    place = lax.axis_index("heads").astype(jnp.int32).reshape(1)

    def shape(*dims, dtype=BF):
        return jax.ShapeDtypeStruct(dims, dtype)

    def swapped(blocks_for):
        return [
            from_partner(block, "nodes", swap_bits[which])
            for block, which in zip(blocks_for, FETCH_ORDER)
        ]

    by_heads = upstream.reshape(-1, depth // width, width).swapaxes(0, 1).reshape(rows, width)
    near, far, near_across, far_across, arriving = gather_pieces(features, by_heads)
    near_pairs = pl.pallas_call(
        near_kernel,
        out_shape=shape(rows, 2 * width),
        in_specs=[SMEM] + [VMEM] * 5,
        out_specs=VMEM,
        compiler_params=params,
        name="project_near",
    )(place, near, near_across, key_weight, value_weight, order_column)
    far_across, arriving = lax.optimization_barrier((far_across, arriving))
    pairs = pl.pallas_call(
        far_kernel,
        out_shape=shape(rows, 2 * width),
        in_specs=[SMEM] + [VMEM] * 6,
        out_specs=VMEM,
        compiler_params=params,
        name="project_far",
    )(place, far, far_across, key_weight, value_weight, order_column, near_pairs)
    others = [from_partner(pairs, "nodes", swap_bits[which]) for which in LOAD_ORDER]
    gathered, asks = pl.pallas_call(
        order_kernel,
        out_shape=(shape(rows, depth), shape(rows, 2 * width)),
        in_specs=[SMEM] + [ANY] * 4 + [VMEM] * 3,
        out_specs=(VMEM,) * 2,
        scratch_shapes=[pltpu.SemaphoreType.DMA((2 * CORES * CORES,))],
        compiler_params=params,
        name="order",
    )(place, near, far, near_across, far_across, query_weight, order_column, arriving)
    mixed, dquery, own_grads, *sent = pl.pallas_call(
        attend_kernel,
        out_shape=(
            shape(rows, width),
            shape(rows, width),
            shape(rows, 2 * width, dtype=F32),
            shape(rows, 2 * width),
            shape(rows, 2 * width),
            shape(rows, 2 * width),
        ),
        in_specs=[SMEM] + [VMEM] * 5,
        out_specs=(VMEM,) * 6,
        compiler_params=params,
        name="attend",
    )(slots, asks, pairs, *others)
    mixed_nodes = pl.pallas_call(
        restore_kernel,
        out_shape=shape(rows, width),
        in_specs=[VMEM] * 2,
        out_specs=VMEM,
        compiler_params=memory(8),
        name="restore",
    )(mixed, order_row)
    returned = swapped(sent)
    dquery_nodes, query_part = pl.pallas_call(
        query_kernel,
        out_shape=(shape(rows, width), shape(depth, width)),
        in_specs=[VMEM] * 3,
        out_specs=(VMEM,) * 2,
        compiler_params=params,
        name="query_grads",
    )(gathered, order_row, dquery)
    weight_part, pair_nodes = pl.pallas_call(
        finish_kernel,
        out_shape=(shape(depth, 3 * width), shape(rows, 2 * width)),
        in_specs=[VMEM] * 7,
        out_specs=(ANY, VMEM),
        scratch_shapes=[
            pltpu.VMEM((depth, 2 * width), BF),
            pltpu.SemaphoreType.DMA((2,)),
        ],
        compiler_params=params,
        name="finish",
    )(gathered, order_row, query_part, own_grads, *returned)
    spread = exchange(weight_part)

    share = rows // lax.axis_size("heads")
    full = depth + width
    keep, give = pl.pallas_call(
        features_kernel,
        out_shape=(shape(rows // CORES, full),) * 2,
        in_specs=[SMEM] + [VMEM] * 6,
        out_specs=(VMEM,) * 2,
        scratch_shapes=[pltpu.VMEM((rows // CORES, 3 * width), BF)],
        compiler_params=memory(6),
        name="features",
    )(place, dquery_nodes, pair_nodes, mixed_nodes, query_weight, key_weight, value_weight)
    got = lax.ppermute(give, "heads", across)
    to_high, to_low = pl.pallas_call(
        far_rows_kernel,
        out_shape=(shape(share // 2, full + width),) * 2,
        in_specs=[VMEM] * 2,
        out_specs=(VMEM,) * 2,
        compiler_params=memory(3),
        name="far_rows",
    )(keep, got)
    from_low = lax.ppermute(to_high, "heads", up)
    from_high = lax.ppermute(to_low, "heads", down)
    spread, from_low, from_high = lax.optimization_barrier((spread, from_low, from_high))
    weight_share = summed_here(spread)
    to_high, to_low = pl.pallas_call(
        near_rows_kernel,
        out_shape=(shape(share, full + 2 * width),) * 2,
        in_specs=[VMEM] * 4,
        out_specs=(VMEM,) * 2,
        compiler_params=memory(3),
        name="near_rows",
    )(keep, got, from_low, from_high)
    from_low = lax.ppermute(to_high, "heads", up)
    from_high = lax.ppermute(to_low, "heads", down)
    weight_grads = exchange(copies_of(weight_share))
    feature_grad, attended = pl.pallas_call(
        collect_kernel,
        out_shape=(shape(share, depth),) * 2,
        in_specs=[SMEM] + [VMEM] * 4,
        out_specs=(VMEM,) * 2,
        compiler_params=memory(3),
        name="collect",
    )(place, keep, got, from_low, from_high)
    piece = depth // 4
    query_grad, key_grad, value_grad = pl.pallas_call(
        widen_kernel,
        grid=(4,),
        out_shape=(shape(depth, width, dtype=F32),) * 3,
        in_specs=[pl.BlockSpec((piece, 3 * width), lambda at: (at, 0))],
        out_specs=(pl.BlockSpec((piece, width), lambda at: (at, 0)),) * 3,
        compiler_params=memory(3),
        name="widen",
    )(weight_grads)
    return attended, feature_grad, query_grad, key_grad, value_grad


def solution(mesh):
    return jax.shard_map(
        local,
        mesh=mesh,
        in_specs=(
            P(("nodes", "heads"), None),
            P("nodes"),
            P(None, "nodes"),
            P(None, "heads"),
            P(None, "heads"),
            P(None, "heads"),
            P(("nodes", "heads"), None),
        ),
        out_specs=(
            P(("nodes", "heads"), None),
            P(("nodes", "heads"), None),
            P(None, "heads"),
            P(None, "heads"),
            P(None, "heads"),
        ),
        check_vma=False,
    )
```
